32 devices in a mesh: gx: 8 (over z, core), gy: 4 (over y, x).
Axes of the slice: x: 2, y: 2, z: 4, core: 2. Of those that a mesh axis runs over, the one named last changes fastest.
Arguments:
- populations: float32 [19, 32, 128, 128], P(None, 'gx', 'gy'), may hold values from 0.5 to 1.5
- solid: int32 [32, 128, 128], P('gx', 'gy'), may hold values 0 or 1
- panel_cell: int32 [8192], P(('gx', 'gy')), may hold values from 0 to 16383
- panel_owner: int32 [8192], P(('gx', 'gy')), may hold values from 0 to 7, as said below
- panel_count: int32 [32], P(('gx', 'gy')), may hold values from 1 to 256, 4096 in all
- panel_area: float32 [3, 8192], P(None, ('gx', 'gy')), may hold values from -4 to 4
- observers: float32 [3, 256], replicated, may hold values from 0 to 288, as said below
- frequencies: float32 [64], replicated, may hold values from 0.01 to 1.5
Outputs:
- populations_out: float32 [19, 32, 128, 128], P(None, 'gx', 'gy')
- patch_spectra: float32 [8, 2, 64, 256], P('gx', None, 'gy')
The draws below stay inside these ranges and needn't reach their ends.
Inputs may be any that keep to these rules, and one draw needn't show every extreme that they name: `panel_owner`: among the 256 slots of each brick every patch is named by exactly 32 slots. `panel_count`: the counts of all bricks sum to 4096 and some brick has all 256 slots live. `observers`: every observer lies 16 or more cells above the lattice: its third coordinate is at least 144.
All inputs are finite; a program needn't handle non-finite values. No bound on the sum of `solid` on one device may be relied on, other than what follows from the above.
Results may differ from the reference program's by a relative error of at most 0.0003.
Values sent between devices are 32-bit elements; how exact they have to be, the bound alone decides.
A program may use at most 64 MiB of HBM per device.

```python
import math
import jax
import jax.numpy as jnp
import numpy as np
from jax import lax

CX = 4
CY = 32
CZ = 128
STEPS = 4
LIST = 256
OBS = 256
FREQS = 64
NX = 32
NY = 128
PATCHES = 8
OWN_CAP = 32
N_GY = 4
DEVICES = 32


def draw_panel_owner(key, part):
    scores = jax.random.randint(key, (DEVICES, LIST), 0, 1 << 20) * LIST + jnp.arange(LIST, dtype=jnp.int32)[None, :]
    ordering = jnp.argsort(scores, axis=1)
    rank_table = jnp.argsort(ordering, axis=1)
    return (rank_table // OWN_CAP).astype(jnp.int32).reshape(DEVICES * LIST)


def draw_observers(key, part):
    key_a, key_b, key_c = jax.random.split(jax.random.fold_in(key, 7), 3)
    across_x = jax.random.uniform(key_a, (OBS,), jnp.float32) * NX
    across_y = jax.random.uniform(key_b, (OBS,), jnp.float32) * NY
    height = CZ + 32.0 + 128.0 * jax.random.uniform(key_c, (OBS,), jnp.float32)
    return jnp.stack([across_x, across_y, height]).astype(jnp.float32)


def set_ends(values, own_key, smallest, largest):
    dims = values.shape
    spot = [jax.random.randint(jax.random.fold_in(own_key, axis), (), 0, dims[axis]) for axis in range(len(dims))]
    values = values.at[tuple(spot)].set(smallest)
    longest = dims.index(max(dims))
    spot[longest] = (spot[longest] + 1) % dims[longest]
    return values.at[tuple(spot)].set(largest)


def steps_of(rng, dims, pieces, smallest, largest):
    factor_of, own = 1.0, jax.random.fold_in(rng, 6)
    for axis_at, parts in pieces:
        heights = jnp.exp(jax.random.uniform(jax.random.fold_in(own, axis_at), (parts,), jnp.float32, smallest / len(pieces), largest / len(pieces)))
        factor_of = factor_of * jnp.repeat(heights, dims[axis_at] // parts).reshape([-1 if axis == axis_at else 1 for axis in range(len(dims))])
    return factor_of


def length_profile(number_of, total, most, skew):
    portions = [(1 << 20) // math.isqrt(rank ** skew) + 1 for rank in range(2, number_of + 1)]
    rest, counts = total - most - (number_of - 1), [1] * (number_of - 1)
    while rest > 0:
        free = [i for i in range(number_of - 1) if counts[i] < most]
        mass, remaining = sum([portions[i] for i in free]), rest
        for i in free:
            extra = min(most - counts[i], max(1, remaining * portions[i] // mass), rest)
            counts[i] = counts[i] + extra
            rest = rest - extra
    return np.array([most] + counts)


def ragged_sizes(own_key, number_of, total, reach, slope):
    if number_of == 2:
        one = jax.random.randint(own_key, (), max(1, total - reach), min(reach, total - 1) + 1)
        return jnp.stack([one, total - one])
    tallies = jnp.asarray(length_profile(number_of, total, reach, slope), jnp.int32)
    pairs = (number_of - 1) // 2
    donor, receiver = tallies[1:1 + 2 * pairs:2], tallies[2:2 + 2 * pairs:2]
    room = jnp.minimum(donor - 1, reach - receiver)
    shifted = jax.random.randint(jax.random.fold_in(own_key, 1), (pairs,), 0, 1 << 20) % (room + 1)
    tallies = tallies.at[1:1 + 2 * pairs:2].set(donor - shifted).at[2:2 + 2 * pairs:2].set(receiver + shifted)
    return tallies[jax.random.permutation(jax.random.fold_in(own_key, 2), number_of)]


def bell_draw(own_key, dims, deviation, bound, pieces=(), held_as=jnp.bfloat16):
    drawn = deviation * jax.random.normal(own_key, dims, jnp.float32)
    if pieces:
        drawn = drawn * steps_of(own_key, dims, pieces, -0.22, 0.18)
    return jnp.clip(drawn, -bound, bound).astype(held_as)


def setup_inputs(seed: int = 0) -> dict:
    key_of = jax.random.split(jax.random.key(seed), 9)
    populations = jnp.clip(0.5 + 1.0 * jax.random.uniform(key_of[0], (19, NX, NY, CZ), jnp.float32) ** steps_of(key_of[0], (19, NX, NY, CZ), ((1, 8), (2, 4)), -0.2, 0.2), 0.5, 1.5)
    solid = set_ends((jax.random.randint(key_of[1], (NX, NY, CZ), 0, 8) < 1).astype(jnp.int32), jax.random.fold_in(key_of[1], 1), 0, 1)
    panel_cell = set_ends(jax.random.randint(key_of[2], (DEVICES * LIST,), 0, CX * CY * CZ), jax.random.fold_in(key_of[2], 1), 0, (CX * CY * CZ) - 1).astype(jnp.int32)
    panel_owner = draw_panel_owner(jax.random.fold_in(key_of[8], 71), 0)
    panel_count = ragged_sizes(key_of[4], DEVICES, DEVICES * LIST // 2, LIST, 2).astype(jnp.int32)
    panel_area = bell_draw(key_of[5], (3, DEVICES * LIST), 1.0, 4.0, ((1, 32),), jnp.float32)
    observers = draw_observers(jax.random.fold_in(key_of[8], 71), 0)
    frequencies = jnp.clip(jnp.exp(jax.random.uniform(key_of[7], (FREQS,), jnp.float32, math.log(0.01), math.log(1.5))), 0.01, 1.5)
    return {"populations": populations, "solid": solid, "panel_cell": panel_cell, "panel_owner": panel_owner, "panel_count": panel_count, "panel_area": panel_area, "observers": observers, "frequencies": frequencies}


VELOCITIES = np.array([[0, 0, 0], [1, 0, 0], [-1, 0, 0], [0, 1, 0], [0, -1, 0], [0, 0, 1], [0, 0, -1], [1, 1, 0], [-1, -1, 0], [1, -1, 0], [-1, 1, 0], [1, 0, 1], [-1, 0, -1], [1, 0, -1], [-1, 0, 1], [0, 1, 1], [0, -1, -1], [0, 1, -1], [0, -1, 1]])
OPPOSITE = [0, 2, 1, 4, 3, 6, 5, 8, 7, 10, 9, 12, 11, 14, 13, 16, 15, 18, 17]
LATTICE_WEIGHTS = [1.0 / 3.0] + [1.0 / 18.0] * 6 + [1.0 / 36.0] * 12
base_density = 19.0
sound_factor = math.sqrt(3.0)

def relaxation():
    along_x = VELOCITIES[:, 0]
    along_y = VELOCITIES[:, 1]
    along_z = VELOCITIES[:, 2]
    constant = np.ones(19)
    raw_list = [constant, along_x, along_y, along_z, along_x * along_x, along_y * along_y, along_z * along_z, along_x * along_y, along_x * along_z, along_y * along_z, along_x * along_x * along_y, along_x * along_x * along_z, along_y * along_y * along_x, along_y * along_y * along_z, along_z * along_z * along_x, along_z * along_z * along_y, along_x * along_x * along_y * along_y, along_x * along_x * along_z * along_z, along_y * along_y * along_z * along_z]
    basis = []
    for vector in raw_list:
        column = np.array(vector) * 1.0
        for previous in basis:
            column = column - previous * (column @ previous) / (previous @ previous)
        basis.append(column)
    matrix = np.stack(basis)
    rate_list = np.array([0.0] * 4 + [1.8] * 6 + [1.4] * 6 + [1.2] * 3)
    inverse = matrix.T / np.sum(matrix * matrix, axis=1)[None, :]
    return inverse @ (rate_list[:, None] * matrix)

def collide(current, solid_mask):
    velocity_table = jnp.asarray(VELOCITIES, jnp.float32)
    weight_table = jnp.asarray(np.array(LATTICE_WEIGHTS), jnp.float32)
    relax_matrix = jnp.asarray(relaxation(), jnp.float32)
    density = lax.optimization_barrier(jnp.sum(current, axis=0))
    momentum = jnp.einsum('qd,qxyz->dxyz', velocity_table, current, precision=lax.Precision.HIGHEST)
    velocity = momentum / density[None]
    projected = jnp.einsum('qd,dxyz->qxyz', velocity_table, velocity, precision=lax.Precision.HIGHEST)
    square = lax.optimization_barrier(jnp.sum(velocity * velocity, axis=0))
    equilibrium = weight_table[:, None, None, None] * density[None] * (1.0 + 3.0 * projected + 4.5 * projected * projected - 1.5 * square[None])
    relaxed = current - jnp.einsum('pq,qxyz->pxyz', relax_matrix, current - equilibrium, precision=lax.Precision.HIGHEST)
    reversed_pops = jnp.stack([current[direction] for direction in OPPOSITE])
    relaxed = jnp.where(solid_mask[None] > 0, reversed_pops, relaxed)
    return (relaxed, density, velocity)

def propagate(relaxed):
    moved = []
    for direction in range(19):
        step_x, step_y, step_z = (int(value) for value in VELOCITIES[direction])
        moved.append(jnp.roll(relaxed[direction], (step_x, step_y, step_z), axis=(0, 1, 2)))
    return jnp.stack(moved)

def panel_terms(sampled_density, sampled_velocity, panel_area, live_mask):
    normal_flux = lax.optimization_barrier(jnp.sum(sampled_velocity * panel_area, axis=0))
    thickness = sampled_density * normal_flux
    loading = (sampled_density - base_density)[None] / 3.0 * panel_area + sampled_density[None] * sampled_velocity * normal_flux[None]
    return jnp.concatenate([thickness[None], loading], axis=0) * live_mask[None]

def window_spectra(series, omega_list):
    step_total = series.shape[0]
    real_part = jnp.zeros((series.shape[1], omega_list.shape[0], series.shape[2]), jnp.float32)
    imag_part = jnp.zeros((series.shape[1], omega_list.shape[0], series.shape[2]), jnp.float32)
    for step_index in range(step_total):
        taper_weight = 0.5 - 0.5 * math.cos(2.0 * math.pi * (step_index + 0.5) / step_total)
        phase_step = omega_list * float(step_index)
        real_part = real_part + (taper_weight * jnp.cos(phase_step))[None, :, None] * series[step_index][:, None, :]
        imag_part = imag_part - (taper_weight * jnp.sin(phase_step))[None, :, None] * series[step_index][:, None, :]
    return (real_part, imag_part)

def green_sum(real_part, imag_part, coords, observers, omega_list):
    offset_x = observers[0][:, None] - coords[0][None, :]
    offset_y = observers[1][:, None] - coords[1][None, :]
    offset_z = observers[2][:, None] - coords[2][None, :]
    distance = jnp.sqrt(offset_x * offset_x + offset_y * offset_y + offset_z * offset_z)
    inverse = 1.0 / distance

    def per_freq(packed):
        omega_now, spec_re, spec_im = packed
        wave_number = omega_now * sound_factor
        radial_re = (offset_x * spec_re[1][None] + offset_y * spec_re[2][None] + offset_z * spec_re[3][None]) * inverse
        radial_im = (offset_x * spec_im[1][None] + offset_y * spec_im[2][None] + offset_z * spec_im[3][None]) * inverse
        amp_re = -omega_now * spec_im[0][None] + radial_re * inverse - wave_number * radial_im
        amp_im = omega_now * spec_re[0][None] + wave_number * radial_re + radial_im * inverse
        phase_angle = wave_number * distance
        cosine_part = jnp.cos(phase_angle)
        sine_part = jnp.sin(phase_angle)
        out_re = lax.optimization_barrier(jnp.sum(inverse * (cosine_part * amp_re + sine_part * amp_im), axis=1))
        out_im = lax.optimization_barrier(jnp.sum(inverse * (cosine_part * amp_im - sine_part * amp_re), axis=1))
        return jnp.stack([out_re, out_im])
    result = lax.map(per_freq, (omega_list, jnp.moveaxis(real_part, 1, 0), jnp.moveaxis(imag_part, 1, 0)))
    return jnp.moveaxis(result, 0, 1)

def reference(populations, solid, panel_cell, panel_owner, panel_count, panel_area, observers, frequencies):
    slot_index = jnp.arange(DEVICES * LIST, dtype=jnp.int32)
    brick_index = slot_index // LIST
    brick_x = brick_index // N_GY
    brick_y = brick_index % N_GY
    local_x = panel_cell // (CY * CZ)
    local_y = panel_cell // CZ % CY
    local_z = panel_cell % CZ
    global_x = brick_x * CX + local_x
    global_y = brick_y * CY + local_y
    coords = jnp.stack([global_x, global_y, local_z]).astype(jnp.float32)
    live_mask = (slot_index % LIST < panel_count[brick_index]).astype(jnp.float32)
    current = populations
    series = []
    for step_index in range(STEPS):
        relaxed, density, velocity = collide(current, solid)
        sampled_density = density[global_x, global_y, local_z]
        sampled_velocity = velocity[:, global_x, global_y, local_z]
        series.append(panel_terms(sampled_density, sampled_velocity, panel_area, live_mask))
        current = propagate(relaxed)
    real_part, imag_part = window_spectra(jnp.stack(series), frequencies)
    grouped = jnp.argsort(panel_owner, stable=True).astype(jnp.int32).reshape(PATCHES, DEVICES * OWN_CAP)

    def per_patch(columns):
        return green_sum(jnp.take(real_part, columns, axis=2), jnp.take(imag_part, columns, axis=2), jnp.take(coords, columns, axis=1), observers, frequencies)
    patch_spectra = lax.map(per_patch, grouped)
    return (current, patch_spectra)
```

```python
import functools
import math

import jax
import jax.numpy as jnp
import numpy as np
from jax import lax
from jax.experimental import pallas as pl
from jax.experimental.pallas import tpu as pltpu
from jax.sharding import PartitionSpec as P

STEPS = 4


VELOCITIES = np.array(
    [
        [0, 0, 0],
        [1, 0, 0],
        [-1, 0, 0],
        [0, 1, 0],
        [0, -1, 0],
        [0, 0, 1],
        [0, 0, -1],
        [1, 1, 0],
        [-1, -1, 0],
        [1, -1, 0],
        [-1, 1, 0],
        [1, 0, 1],
        [-1, 0, -1],
        [1, 0, -1],
        [-1, 0, 1],
        [0, 1, 1],
        [0, -1, -1],
        [0, 1, -1],
        [0, -1, 1],
    ]
)
OPPOSITE = [0, 2, 1, 4, 3, 6, 5, 8, 7, 10, 9, 12, 11, 14, 13, 16, 15, 18, 17]
LATTICE_WEIGHTS = [1.0 / 3.0] + [1.0 / 18.0] * 6 + [1.0 / 36.0] * 12


def moment_basis():
    along_x = VELOCITIES[:, 0]
    along_y = VELOCITIES[:, 1]
    along_z = VELOCITIES[:, 2]
    constant = np.ones(19)
    raw_list = [
        constant,
        along_x,
        along_y,
        along_z,
        along_x * along_x,
        along_y * along_y,
        along_z * along_z,
        along_x * along_y,
        along_x * along_z,
        along_y * along_z,
        along_x * along_x * along_y,
        along_x * along_x * along_z,
        along_y * along_y * along_x,
        along_y * along_y * along_z,
        along_z * along_z * along_x,
        along_z * along_z * along_y,
        along_x * along_x * along_y * along_y,
        along_x * along_x * along_z * along_z,
        along_y * along_y * along_z * along_z,
    ]
    basis = []
    for vector in raw_list:
        column = np.array(vector) * 1.0
        for previous in basis:
            column = column - previous * (column @ previous) / (previous @ previous)
        basis.append(column)
    matrix = np.stack(basis)
    return matrix


PAIRS = [1, 3, 5, 7, 9, 11, 13, 15, 17]
PLUS_X = [i for i in range(19) if VELOCITIES[i][0] == 1]
MINUS_X = [i for i in range(19) if VELOCITIES[i][0] == -1]
PLUS_Y = [i for i in range(19) if VELOCITIES[i][1] == 1]
MINUS_Y = [i for i in range(19) if VELOCITIES[i][1] == -1]
CORNERS = [(7, 1, 1), (8, -1, -1), (9, 1, -1), (10, -1, 1)]
CLASS_OF_PAIR = [1, 2, 3, 4, 4, 5, 5, 6, 6]
CLASS_MEMBER = [0, 1, 3, 5, 7, 11, 15]
MOMENTS = moment_basis()
MESH = pl.DeviceIdType.MESH


def signed_sum(terms):
    total = None
    for sign, value in terms:
        if total is None:
            total = value if sign > 0 else -value
        else:
            total = total + value if sign > 0 else total - value
    return total


def along(axis, odd):
    return signed_sum(
        [
            (VELOCITIES[i][axis], odd[n])
            for n, i in enumerate(PAIRS)
            if VELOCITIES[i][axis] != 0
        ]
    )


def tree_sum(values):
    values = list(values)
    while len(values) > 1:
        values = [
            values[i] + values[i + 1] if i + 1 < len(values) else values[i]
            for i in range(0, len(values), 2)
        ]
    return values[0]


def collide_tile(f, solid):
    even = [f[i] + f[i + 1] for i in PAIRS]
    odd = [f[i] - f[i + 1] for i in PAIRS]
    rho = tree_sum([f[0]] + even)
    inverse = 1.0 / rho
    u = [along(axis, odd) * inverse for axis in range(3)]
    base = 1.0 - 1.5 * (u[0] * u[0] + u[1] * u[1] + u[2] * u[2])
    scaled = {w: rho * w for w in (1.0 / 9.0, 1.0 / 18.0)}
    rest = f[0] - (rho * (1.0 / 3.0)) * base
    d_even, d_odd = [], []
    for n, i in enumerate(PAIRS):
        weight = scaled[1.0 / 9.0] if i < 7 else scaled[1.0 / 18.0]
        cu = signed_sum([(VELOCITIES[i][a], u[a]) for a in range(3) if VELOCITIES[i][a] != 0])
        d_even.append(even[n] - weight * (base + 4.5 * (cu * cu)))
        d_odd.append(odd[n] - weight * (3.0 * cu))
    mean = tree_sum([rest] + d_even) * (1.8 / 19.0)
    drift = [along(axis, d_odd) * (1.4 / 10.0) for axis in range(3)]
    classes = [rest] + [
        tree_sum([d_even[n] for n in range(9) if CLASS_OF_PAIR[n] == c]) for c in range(1, 7)
    ]
    high = [mean] * 7
    for k in range(16, 19):
        row = MOMENTS[k]
        norm = float(row @ row)
        picked = [(c, float(row[m])) for c, m in enumerate(CLASS_MEMBER) if abs(row[m]) > 1e-9]
        moment = tree_sum([classes[c] * value for c, value in picked])
        for c, value in picked:
            high[c] = high[c] + moment * (0.6 * value / norm)
    relaxed = [None] * 19
    relaxed[0] = f[0] - (1.8 * rest - high[0])
    for n, i in enumerate(PAIRS):
        part_e = 0.9 * d_even[n] - high[CLASS_OF_PAIR[n]]
        part_o = 0.7 * d_odd[n] - signed_sum(
            [(VELOCITIES[i][a], drift[a]) for a in range(3) if VELOCITIES[i][a] != 0]
        )
        relaxed[i] = jnp.where(solid, f[i + 1], f[i] - (part_e + part_o))
        relaxed[i + 1] = jnp.where(solid, f[i], f[i + 1] - (part_e - part_o))
    relaxed[0] = jnp.where(solid, f[0], relaxed[0])
    return relaxed, rho, u


def flow_kernel(
    count_x,
    count_y,
    f_ref,
    solid_ref,
    meta_ref,
    out_ref,
    panels_ref,
    grid,
    fields,
    send_x,
    recv_x,
    send_y,
    recv_y,
    send_c,
    recv_c,
    payload,
    panels,
    step_send,
    step_recv,
    panel_send,
    panel_recv,
    own_sem,
):
    width_x, width_y, depth_z = solid_ref.shape
    slots = meta_ref.shape[1]
    capacity = slots // count_x
    total = count_x * count_y
    me_x, me_y = lax.axis_index("gx"), lax.axis_index("gy")
    me = me_x * count_y + me_y
    tiles_y = width_y // 8

    barrier = pltpu.get_barrier_semaphore()

    def greet(d, carry):
        @pl.when(d != me)
        def _():
            pl.semaphore_signal(
                barrier,
                inc=1,
                device_id=(d // count_y, d % count_y),
                device_id_type=MESH,
            )

        return carry

    lax.fori_loop(0, total, greet, 0)

    right_x, left_x = lax.rem(me_x + 1, count_x), lax.rem(me_x + count_x - 1, count_x)
    right_y, left_y = lax.rem(me_y + 1, count_y), lax.rem(me_y + count_y - 1, count_y)

    def side(step, n):
        if n < 2:
            source, target = send_x.at[step, n], recv_x.at[step, n]
            place = (right_x if n == 0 else left_x, me_y)
        elif n < 4:
            source, target = send_y.at[step, n - 2], recv_y.at[step, n - 2]
            place = (me_x, right_y if n == 2 else left_y)
        else:
            _, step_x, step_y = CORNERS[n - 4]
            source, target = send_c.at[step, n - 4], recv_c.at[step, n - 4]
            place = (right_x if step_x > 0 else left_x, right_y if step_y > 0 else left_y)
        return pltpu.make_async_remote_copy(
            src_ref=source,
            dst_ref=target,
            send_sem=step_send.at[step, n],
            recv_sem=step_recv.at[step, n],
            device_id=place,
            device_id_type=MESH,
        )

    def pulled(buffer, i, x, row):
        step_x, step_y, step_z = (int(v) for v in VELOCITIES[i])
        value = grid[buffer, i, x + 1 - step_x, pl.ds(row + 8 - step_y, 8), :]
        if step_z:
            value = pltpu.roll(value, step_z % depth_z, axis=1)
        return value

    def collide_slab(step, x):
        for tile in range(tiles_y):
            row = tile * 8
            if step == 0:
                f = [f_ref[i, x, pl.ds(row, 8), :] for i in range(19)]
            else:
                f = [pulled((step - 1) % 2, i, x, row) for i in range(19)]
            relaxed, rho, u = collide_tile(f, solid_ref[x, pl.ds(row, 8), :] > 0)
            for i in range(19):
                grid[step % 2, i, x + 1, pl.ds(row + 8, 8), :] = relaxed[i]
            for n, value in enumerate([rho] + u):
                fields[n, x, pl.ds(row, 8), :] = value

    def arrive(step):
        buffer = step % 2
        for n in range(8):
            side(step, n).wait_recv()
        for k in range(5):
            grid[buffer, PLUS_X[k], 0, pl.ds(8, width_y), :] = recv_x[step, 0, k]
            grid[buffer, MINUS_X[k], width_x + 1, pl.ds(8, width_y), :] = recv_x[step, 1, k]
        for k in range(5):
            for x in range(width_x):
                line = pl.ds(k * width_x + x, 1)
                grid[buffer, PLUS_Y[k], x + 1, pl.ds(7, 1), :] = recv_y[step, 0, line, :]
                grid[buffer, MINUS_Y[k], x + 1, pl.ds(width_y + 8, 1), :] = recv_y[step, 1, line, :]
        for n, (i, step_x, step_y) in enumerate(CORNERS):
            x = 0 if step_x > 0 else width_x + 1
            row = 7 if step_y > 0 else width_y + 8
            grid[buffer, i, x, pl.ds(row, 1), :] = recv_c[step, n, pl.ds(0, 1), :]

    cells = lax.broadcasted_iota(jnp.int32, (depth_z, slots), 0).astype(jnp.float32)
    at_z = jnp.where(cells == meta_ref[pl.ds(6, 1), :], 1.0, 0.0).astype(jnp.bfloat16)
    lines = lax.broadcasted_iota(jnp.int32, (width_x * width_y, slots), 0).astype(jnp.float32)
    row_of = lax.broadcasted_iota(jnp.int32, (8, slots), 0)
    lane_of = lax.broadcasted_iota(jnp.int32, (8, 128), 1)

    def sample(step):
        data = fields[...].reshape(4 * width_x * width_y, depth_z)
        high = data.astype(jnp.bfloat16)
        left = data - high.astype(jnp.float32)
        middle = left.astype(jnp.bfloat16)
        low = (left - middle.astype(jnp.float32)).astype(jnp.bfloat16)
        picked = sum(
            jnp.dot(part, at_z, preferred_element_type=jnp.float32) for part in (high, middle, low)
        )
        at_line = lines == meta_ref[pl.ds(3, 1), :]
        count = width_x * width_y
        rho, ux, uy, uz = (
            jnp.sum(
                jnp.where(at_line, picked[n * count : (n + 1) * count], 0.0), axis=0, keepdims=True
            )
            for n in range(4)
        )
        area = [meta_ref[pl.ds(a, 1), :] for a in range(3)]
        live = meta_ref[pl.ds(7, 1), :]
        flux = ux * area[0] + uy * area[1] + uz * area[2]
        terms = [rho * flux] + [
            (rho - 19.0) / 3.0 * a + rho * v * flux for a, v in zip(area, (ux, uy, uz))
        ]
        block = meta_ref[...] if step == 0 else jnp.zeros((8, slots), jnp.float32)
        for n in range(4):
            block = jnp.where(row_of == n, terms[n] * live, block)
        for q in range(count_x):
            start = q * capacity
            part = block[:, start // 128 * 128 : start // 128 * 128 + 128]
            shift = (step * capacity - start) % 128
            if shift:
                part = pltpu.roll(part, shift, axis=1)
            here = (lane_of >= step * capacity) & (lane_of < (step + 1) * capacity)
            old = payload[q] if step else jnp.zeros((8, 128), jnp.float32)
            payload[q] = jnp.where(here, part, old)

    def panel_copy(d):
        return pltpu.make_async_remote_copy(
            src_ref=payload.at[d // count_y],
            dst_ref=panels.at[me],
            send_sem=panel_send.at[d],
            recv_sem=panel_recv.at[me],
            device_id=(d // count_y, d % count_y),
            device_id_type=MESH,
        )

    def panel_arrival(d):
        return pltpu.make_async_remote_copy(
            src_ref=payload.at[d // count_y],
            dst_ref=panels.at[d],
            send_sem=panel_send.at[d],
            recv_sem=panel_recv.at[d],
            device_id=(d // count_y, d % count_y),
            device_id_type=MESH,
        )

    def for_others(body):
        def one(d, carry):
            @pl.when(d != me)
            def _():
                body(d)

            return carry

        lax.fori_loop(0, total, one, 0)

    for step in range(STEPS):
        buffer = step % 2
        if step:
            arrive(step - 1)

        def outer(n, carry):
            collide_slab(step, n * (width_x - 1))
            return carry

        lax.fori_loop(0, 2, outer, 0)
        for k in range(5):
            send_x[step, 0, k] = grid[buffer, PLUS_X[k], width_x, pl.ds(8, width_y), :]
            send_x[step, 1, k] = grid[buffer, MINUS_X[k], 1, pl.ds(8, width_y), :]
        for n, (i, step_x, step_y) in enumerate(CORNERS):
            x = width_x if step_x > 0 else 1
            row = width_y + 7 if step_y > 0 else 8
            line = grid[buffer, i, x, pl.ds(row, 1), :]
            send_c[step, n] = jnp.broadcast_to(line, (8, depth_z))
        if step == 0:
            pl.semaphore_wait(barrier, total - 1)
        for n in (0, 1, 4, 5, 6, 7):
            side(step, n).start()

        def inner(x, carry):
            collide_slab(step, x)
            return carry

        lax.fori_loop(1, width_x - 1, inner, 0)
        for k in range(5):
            for x in range(width_x):
                line = pl.ds(k * width_x + x, 1)
                send_y[step, 0, line, :] = grid[
                    buffer, PLUS_Y[k], x + 1, pl.ds(width_y + 7, 1), :
                ]
                send_y[step, 1, line, :] = grid[buffer, MINUS_Y[k], x + 1, pl.ds(8, 1), :]
        for n in (2, 3):
            side(step, n).start()
        sample(step)

    for_others(lambda d: panel_copy(d).start())
    own = pltpu.make_async_copy(payload.at[me_x], panels.at[me], own_sem)
    own.start()
    arrive(STEPS - 1)

    def final(x, carry):
        for tile in range(tiles_y):
            for i in range(19):
                out_ref[i, x, pl.ds(tile * 8, 8), :] = pulled((STEPS - 1) % 2, i, x, tile * 8)
        return carry

    lax.fori_loop(0, width_x, final, 0)
    own.wait()
    for_others(lambda d: panel_arrival(d).wait_recv())
    panels_ref[...] = panels[...]
    for_others(lambda d: panel_copy(d).wait_send())
    for step in range(STEPS):
        for n in range(8):
            side(step, n).wait_send()


SIN_POLY = (4.44288292, -7.30824569, 3.60635422, -0.84611165, 0.10982452)
COS_POLY = (1.4142135, -6.97885095, 5.73946038, -1.88355791, 0.31068803)


def horner(poly, x):
    value = poly[-1] * x + poly[-2]
    for coefficient in poly[-3::-1]:
        value = value * x + coefficient
    return value


def green_kernel(
    capacity, count_ref, turn_ref, inverse_ref, table_ref, coords_ref, seen_ref, out_ref, sums
):
    freqs = turn_ref.shape[0]
    sources = count_ref.shape[0]
    observers = seen_ref.shape[1]
    sums[...] = jnp.zeros_like(sums)

    def tile(source, part):
        base = pl.multiple_of(source * capacity + part * 8, 8)
        table = table_ref[pl.ds(base, 8), :]
        coords = coords_ref[pl.ds(base, 8), :]
        offset = [seen_ref[pl.ds(a, 1), :] - coords[:, 4 + a : 5 + a] for a in range(3)]
        distance = jnp.sqrt(
            offset[0] * offset[0] + offset[1] * offset[1] + offset[2] * offset[2]
        )
        inverse = 1.0 / distance
        toward = [value * inverse for value in offset]
        for f in range(freqs):
            column = [
                jnp.broadcast_to(table[:, f * 8 + c : f * 8 + c + 1], (8, observers))
                for c in range(8)
            ]
            turns = distance * turn_ref[f]
            turns = turns - jnp.round(turns)
            square = turns * turns
            half_sin = turns * horner(SIN_POLY, square)
            half_cos = horner(COS_POLY, square)
            cosine = 1.0 - half_sin * half_sin
            sine = half_sin * half_cos
            near = inverse * inverse_ref[f]
            radial_re = toward[0] * column[0] + toward[1] * column[1] + toward[2] * column[2]
            radial_im = toward[0] * column[3] + toward[1] * column[4] + toward[2] * column[5]
            amp_re = radial_re * near - (radial_im + column[7])
            amp_im = radial_im * near + (radial_re + column[6])
            sums[2 * f] += inverse * (cosine * amp_re + sine * amp_im)
            sums[2 * f + 1] += inverse * (cosine * amp_im - sine * amp_re)

    def one_source(source, carry):
        def one_part(part, inner):
            tile(source, part)
            return inner

        lax.fori_loop(0, (count_ref[source] + 7) // 8, one_part, 0)
        return carry

    lax.fori_loop(0, sources, one_source, 0)
    for f in range(freqs):
        for part in range(2):
            out_ref[part, pl.ds(f, 1), :] = jnp.sum(sums[2 * f + part], axis=0, keepdims=True)


def spectrum_table(own_list):
    steps = np.arange(STEPS)
    taper = jnp.asarray(0.5 - 0.5 * np.cos(2.0 * np.pi * (steps + 0.5) / STEPS), jnp.float32)
    phase = own_list[None, :] * jnp.asarray(steps, jnp.float32)[:, None]
    real, imag = taper[:, None] * jnp.cos(phase), -taper[:, None] * jnp.sin(phase)
    wave = own_list * math.sqrt(3.0)
    masks = np.zeros((4, 8, 8), np.float32)
    for a in range(3):
        masks[0, 1 + a, a] = 1.0
        masks[1, 1 + a, 3 + a] = 1.0
    masks[2, 0, 6] = 1.0
    masks[3, 0, 7] = 1.0
    parts = (real * wave, imag * wave, real * own_list, imag * own_list)
    table = sum(
        value[:, None, :, None] * jnp.asarray(mask)[None, :, None, :]
        for value, mask in zip(parts, masks)
    )
    return table.reshape(STEPS * 8, own_list.shape[0] * 8)


def local(
    populations, solid, panel_cell, panel_owner, panel_count, panel_area, observers, frequencies
):
    width_x, width_y, depth_z = solid.shape
    slots = panel_cell.shape[0]
    count_x, count_y = lax.axis_size("gx"), lax.axis_size("gy")
    total = count_x * count_y
    capacity = slots // count_x
    own_freq = frequencies.shape[0] // count_y
    brick_x, brick_y = lax.axis_index("gx"), lax.axis_index("gy")
    line = panel_cell // depth_z
    slot = jnp.arange(slots, dtype=jnp.int32)
    meta = jnp.stack(
        [
            panel_area[0],
            panel_area[1],
            panel_area[2],
            line.astype(jnp.float32),
            (brick_x * width_x + line // width_y).astype(jnp.float32),
            (brick_y * width_y + line % width_y).astype(jnp.float32),
            (panel_cell % depth_z).astype(jnp.float32),
            (slot < panel_count[0]).astype(jnp.float32),
        ]
    )
    earlier = (panel_owner[:, None] == panel_owner[None, :]) & (slot[:, None] < slot[None, :])
    position = panel_owner * capacity + jnp.sum(earlier.astype(jnp.int32), axis=0)
    meta = jnp.sum(
        jnp.where(position[None, :, None] == slot[None, None, :], meta[:, :, None], 0.0), axis=1
    )
    f32 = jnp.float32
    vmem = pl.BlockSpec(memory_space=pltpu.VMEM)
    smem = pl.BlockSpec(memory_space=pltpu.SMEM)
    rows_y = -(-5 * width_x // 8) * 8
    flow = pl.pallas_call(
        functools.partial(flow_kernel, count_x, count_y),
        out_shape=(
            jax.ShapeDtypeStruct(populations.shape, f32),
            jax.ShapeDtypeStruct((total, 8, 128), f32),
        ),
        in_specs=[vmem] * 3,
        out_specs=(vmem, vmem),
        scratch_shapes=[
            pltpu.VMEM((2, 19, width_x + 2, width_y + 16, depth_z), f32),
            pltpu.VMEM((4, width_x, width_y, depth_z), f32),
            pltpu.VMEM((STEPS, 2, 5, width_y, depth_z), f32),
            pltpu.VMEM((STEPS, 2, 5, width_y, depth_z), f32),
            pltpu.VMEM((STEPS, 2, rows_y, depth_z), f32),
            pltpu.VMEM((STEPS, 2, rows_y, depth_z), f32),
            pltpu.VMEM((STEPS, 4, 8, depth_z), f32),
            pltpu.VMEM((STEPS, 4, 8, depth_z), f32),
            pltpu.VMEM((count_x, 8, 128), f32),
            pltpu.VMEM((total, 8, 128), f32),
            pltpu.SemaphoreType.DMA((STEPS, 8)),
            pltpu.SemaphoreType.DMA((STEPS, 8)),
            pltpu.SemaphoreType.DMA((total,)),
            pltpu.SemaphoreType.DMA((total,)),
            pltpu.SemaphoreType.DMA,
        ],
        compiler_params=pltpu.CompilerParams(
            collective_id=0, has_side_effects=True, vmem_limit_bytes=40 * 1024 * 1024
        ),
        name="flow",
    )
    current, panels = flow(populations, solid, meta)

    own_list = lax.dynamic_slice_in_dim(frequencies, brick_y * own_freq, own_freq)
    wave = own_list * math.sqrt(3.0)
    live_in = jnp.sum(panels[:, 7, :capacity], axis=1).astype(jnp.int32)
    samples = panels[:, :, : STEPS * capacity].reshape(total, 8, STEPS, capacity)
    samples = samples.transpose(0, 3, 2, 1).reshape(total * capacity, STEPS * 8)
    table = jnp.dot(samples, spectrum_table(own_list), precision=lax.Precision.HIGHEST)
    spectra = pl.pallas_call(
        functools.partial(green_kernel, capacity),
        out_shape=jax.ShapeDtypeStruct((2, own_freq, observers.shape[1]), f32),
        in_specs=[smem] * 3 + [vmem] * 3,
        out_specs=vmem,
        scratch_shapes=[pltpu.VMEM((2 * own_freq, 8, observers.shape[1]), f32)],
        compiler_params=pltpu.CompilerParams(vmem_limit_bytes=40 * 1024 * 1024),
        name="green",
    )(live_in, wave * (0.5 / math.pi), 1.0 / wave, table, samples, observers)
    return (current, spectra[None])


def solution(mesh):
    return jax.shard_map(
        local,
        mesh=mesh,
        in_specs=(
            P(None, "gx", "gy", None),
            P("gx", "gy", None),
            P(("gx", "gy")),
            P(("gx", "gy")),
            P(("gx", "gy")),
            P(None, ("gx", "gy")),
            P(),
            P(),
        ),
        out_specs=(P(None, "gx", "gy", None), P("gx", None, "gy", None)),
        check_vma=False,
    )
```

```python
import functools
import math

import jax
import jax.numpy as jnp
import numpy as np
from jax import lax
from jax.experimental import pallas as pl
from jax.experimental.pallas import tpu as pltpu
from jax.sharding import PartitionSpec as P

STEPS = 4


VELOCITIES = np.array(
    [
        [0, 0, 0],
        [1, 0, 0],
        [-1, 0, 0],
        [0, 1, 0],
        [0, -1, 0],
        [0, 0, 1],
        [0, 0, -1],
        [1, 1, 0],
        [-1, -1, 0],
        [1, -1, 0],
        [-1, 1, 0],
        [1, 0, 1],
        [-1, 0, -1],
        [1, 0, -1],
        [-1, 0, 1],
        [0, 1, 1],
        [0, -1, -1],
        [0, 1, -1],
        [0, -1, 1],
    ]
)
OPPOSITE = [0, 2, 1, 4, 3, 6, 5, 8, 7, 10, 9, 12, 11, 14, 13, 16, 15, 18, 17]
LATTICE_WEIGHTS = [1.0 / 3.0] + [1.0 / 18.0] * 6 + [1.0 / 36.0] * 12


def moment_basis():
    along_x = VELOCITIES[:, 0]
    along_y = VELOCITIES[:, 1]
    along_z = VELOCITIES[:, 2]
    constant = np.ones(19)
    raw_list = [
        constant,
        along_x,
        along_y,
        along_z,
        along_x * along_x,
        along_y * along_y,
        along_z * along_z,
        along_x * along_y,
        along_x * along_z,
        along_y * along_z,
        along_x * along_x * along_y,
        along_x * along_x * along_z,
        along_y * along_y * along_x,
        along_y * along_y * along_z,
        along_z * along_z * along_x,
        along_z * along_z * along_y,
        along_x * along_x * along_y * along_y,
        along_x * along_x * along_z * along_z,
        along_y * along_y * along_z * along_z,
    ]
    basis = []
    for vector in raw_list:
        column = np.array(vector) * 1.0
        for previous in basis:
            column = column - previous * (column @ previous) / (previous @ previous)
        basis.append(column)
    matrix = np.stack(basis)
    return matrix


PAIRS = [1, 3, 5, 7, 9, 11, 13, 15, 17]
PLUS_X = [i for i in range(19) if VELOCITIES[i][0] == 1]
MINUS_X = [i for i in range(19) if VELOCITIES[i][0] == -1]
PLUS_Y = [i for i in range(19) if VELOCITIES[i][1] == 1]
MINUS_Y = [i for i in range(19) if VELOCITIES[i][1] == -1]
CORNERS = [(7, 1, 1), (8, -1, -1), (9, 1, -1), (10, -1, 1)]
CLASS_OF_PAIR = [1, 2, 3, 4, 4, 5, 5, 6, 6]
CLASS_MEMBER = [0, 1, 3, 5, 7, 11, 15]
MOMENTS = moment_basis()
MESH = pl.DeviceIdType.MESH


def signed_sum(terms):
    total = None
    for sign, value in terms:
        if total is None:
            total = value if sign > 0 else -value
        else:
            total = total + value if sign > 0 else total - value
    return total


def along(axis, odd):
    return signed_sum(
        [
            (VELOCITIES[i][axis], odd[n])
            for n, i in enumerate(PAIRS)
            if VELOCITIES[i][axis] != 0
        ]
    )


def tree_sum(values):
    values = list(values)
    while len(values) > 1:
        values = [
            values[i] + values[i + 1] if i + 1 < len(values) else values[i]
            for i in range(0, len(values), 2)
        ]
    return values[0]


def collide_tile(f, solid):
    even = [f[i] + f[i + 1] for i in PAIRS]
    odd = [f[i] - f[i + 1] for i in PAIRS]
    rho = tree_sum([f[0]] + even)
    inverse = 1.0 / rho
    u = [along(axis, odd) * inverse for axis in range(3)]
    base = 1.0 - 1.5 * (u[0] * u[0] + u[1] * u[1] + u[2] * u[2])
    scaled = {w: rho * w for w in (1.0 / 9.0, 1.0 / 18.0)}
    rest = f[0] - (rho * (1.0 / 3.0)) * base
    d_even, d_odd = [], []
    for n, i in enumerate(PAIRS):
        weight = scaled[1.0 / 9.0] if i < 7 else scaled[1.0 / 18.0]
        cu = signed_sum([(VELOCITIES[i][a], u[a]) for a in range(3) if VELOCITIES[i][a] != 0])
        d_even.append(even[n] - weight * (base + 4.5 * (cu * cu)))
        d_odd.append(odd[n] - weight * (3.0 * cu))
    mean = tree_sum([rest] + d_even) * (1.8 / 19.0)
    drift = [along(axis, d_odd) * (1.4 / 10.0) for axis in range(3)]
    classes = [rest] + [
        tree_sum([d_even[n] for n in range(9) if CLASS_OF_PAIR[n] == c]) for c in range(1, 7)
    ]
    high = [mean] * 7
    for k in range(16, 19):
        row = MOMENTS[k]
        norm = float(row @ row)
        picked = [(c, float(row[m])) for c, m in enumerate(CLASS_MEMBER) if abs(row[m]) > 1e-9]
        moment = tree_sum([classes[c] * value for c, value in picked])
        for c, value in picked:
            high[c] = high[c] + moment * (0.6 * value / norm)
    relaxed = [None] * 19
    relaxed[0] = f[0] - (1.8 * rest - high[0])
    for n, i in enumerate(PAIRS):
        part_e = 0.9 * d_even[n] - high[CLASS_OF_PAIR[n]]
        part_o = 0.7 * d_odd[n] - signed_sum(
            [(VELOCITIES[i][a], drift[a]) for a in range(3) if VELOCITIES[i][a] != 0]
        )
        relaxed[i] = jnp.where(solid, f[i + 1], f[i] - (part_e + part_o))
        relaxed[i + 1] = jnp.where(solid, f[i], f[i + 1] - (part_e - part_o))
    relaxed[0] = jnp.where(solid, f[0], relaxed[0])
    return relaxed, rho, u


def flow_kernel(
    count_x,
    count_y,
    f_ref,
    solid_ref,
    meta_ref,
    out_ref,
    panels_ref,
    grid,
    fields,
    send_x,
    recv_x,
    send_y,
    recv_y,
    send_c,
    recv_c,
    payload,
    panels,
    step_send,
    step_recv,
    panel_send,
    panel_recv,
    own_sem,
):
    width_x, width_y, depth_z = solid_ref.shape
    slots = meta_ref.shape[1]
    capacity = slots // count_x
    total = count_x * count_y
    me_x, me_y = lax.axis_index("gx"), lax.axis_index("gy")
    me = me_x * count_y + me_y
    tiles_y = width_y // 8

    barrier = pltpu.get_barrier_semaphore()

    def greet(d, carry):
        @pl.when(d != me)
        def _():
            pl.semaphore_signal(
                barrier,
                inc=1,
                device_id=(d // count_y, d % count_y),
                device_id_type=MESH,
            )

        return carry

    lax.fori_loop(0, total, greet, 0)

    right_x, left_x = lax.rem(me_x + 1, count_x), lax.rem(me_x + count_x - 1, count_x)
    right_y, left_y = lax.rem(me_y + 1, count_y), lax.rem(me_y + count_y - 1, count_y)

    def side(step, n):
        if n < 2:
            source, target = send_x.at[step, n], recv_x.at[step, n]
            place = (right_x if n == 0 else left_x, me_y)
        elif n < 4:
            source, target = send_y.at[step, n - 2], recv_y.at[step, n - 2]
            place = (me_x, right_y if n == 2 else left_y)
        else:
            _, step_x, step_y = CORNERS[n - 4]
            source, target = send_c.at[step, n - 4], recv_c.at[step, n - 4]
            place = (right_x if step_x > 0 else left_x, right_y if step_y > 0 else left_y)
        return pltpu.make_async_remote_copy(
            src_ref=source,
            dst_ref=target,
            send_sem=step_send.at[step, n],
            recv_sem=step_recv.at[step, n],
            device_id=place,
            device_id_type=MESH,
        )

    def pulled(buffer, i, x, row):
        step_x, step_y, step_z = (int(v) for v in VELOCITIES[i])
        value = grid[buffer, i, x + 1 - step_x, pl.ds(row + 8 - step_y, 8), :]
        if step_z:
            value = pltpu.roll(value, step_z % depth_z, axis=1)
        return value

    def collide_slab(step, x):
        for tile in range(tiles_y):
            row = tile * 8
            if step == 0:
                f = [f_ref[i, x, pl.ds(row, 8), :] for i in range(19)]
            else:
                f = [pulled((step - 1) % 2, i, x, row) for i in range(19)]
            relaxed, rho, u = collide_tile(f, solid_ref[x, pl.ds(row, 8), :] > 0)
            for i in range(19):
                grid[step % 2, i, x + 1, pl.ds(row + 8, 8), :] = relaxed[i]
            for n, value in enumerate([rho] + u):
                fields[n, x, pl.ds(row, 8), :] = value

    def arrive(step):
        buffer = step % 2
        for n in range(8):
            side(step, n).wait_recv()
        for k in range(5):
            grid[buffer, PLUS_X[k], 0, pl.ds(8, width_y), :] = recv_x[step, 0, k]
            grid[buffer, MINUS_X[k], width_x + 1, pl.ds(8, width_y), :] = recv_x[step, 1, k]
        for k in range(5):
            for x in range(width_x):
                line = pl.ds(k * width_x + x, 1)
                grid[buffer, PLUS_Y[k], x + 1, pl.ds(7, 1), :] = recv_y[step, 0, line, :]
                grid[buffer, MINUS_Y[k], x + 1, pl.ds(width_y + 8, 1), :] = recv_y[step, 1, line, :]
        for n, (i, step_x, step_y) in enumerate(CORNERS):
            x = 0 if step_x > 0 else width_x + 1
            row = 7 if step_y > 0 else width_y + 8
            grid[buffer, i, x, pl.ds(row, 1), :] = recv_c[step, n, pl.ds(0, 1), :]

    cells = lax.broadcasted_iota(jnp.int32, (depth_z, slots), 0).astype(jnp.float32)
    at_z = jnp.where(cells == meta_ref[pl.ds(6, 1), :], 1.0, 0.0).astype(jnp.bfloat16)
    lines = lax.broadcasted_iota(jnp.int32, (width_x * width_y, slots), 0).astype(jnp.float32)
    row_of = lax.broadcasted_iota(jnp.int32, (8, slots), 0)
    lane_of = lax.broadcasted_iota(jnp.int32, (8, 128), 1)

    def sample(step):
        data = fields[...].reshape(4 * width_x * width_y, depth_z)
        high = data.astype(jnp.bfloat16)
        left = data - high.astype(jnp.float32)
        middle = left.astype(jnp.bfloat16)
        low = (left - middle.astype(jnp.float32)).astype(jnp.bfloat16)
        picked = sum(
            jnp.dot(part, at_z, preferred_element_type=jnp.float32) for part in (high, middle, low)
        )
        at_line = lines == meta_ref[pl.ds(3, 1), :]
        count = width_x * width_y
        rho, ux, uy, uz = (
            jnp.sum(
                jnp.where(at_line, picked[n * count : (n + 1) * count], 0.0), axis=0, keepdims=True
            )
            for n in range(4)
        )
        area = [meta_ref[pl.ds(a, 1), :] for a in range(3)]
        live = meta_ref[pl.ds(7, 1), :]
        flux = ux * area[0] + uy * area[1] + uz * area[2]
        terms = [rho * flux] + [
            (rho - 19.0) / 3.0 * a + rho * v * flux for a, v in zip(area, (ux, uy, uz))
        ]
        block = meta_ref[...] if step == 0 else jnp.zeros((8, slots), jnp.float32)
        for n in range(4):
            block = jnp.where(row_of == n, terms[n] * live, block)
        for q in range(count_x):
            start = q * capacity
            part = block[:, start // 128 * 128 : start // 128 * 128 + 128]
            shift = (step * capacity - start) % 128
            if shift:
                part = pltpu.roll(part, shift, axis=1)
            here = (lane_of >= step * capacity) & (lane_of < (step + 1) * capacity)
            old = payload[q] if step else jnp.zeros((8, 128), jnp.float32)
            payload[q] = jnp.where(here, part, old)

    def panel_copy(d):
        return pltpu.make_async_remote_copy(
            src_ref=payload.at[d // count_y],
            dst_ref=panels.at[me],
            send_sem=panel_send.at[d],
            recv_sem=panel_recv.at[me],
            device_id=(d // count_y, d % count_y),
            device_id_type=MESH,
        )

    def panel_arrival(d):
        return pltpu.make_async_remote_copy(
            src_ref=payload.at[d // count_y],
            dst_ref=panels.at[d],
            send_sem=panel_send.at[d],
            recv_sem=panel_recv.at[d],
            device_id=(d // count_y, d % count_y),
            device_id_type=MESH,
        )

    def for_others(body):
        def one(d, carry):
            @pl.when(d != me)
            def _():
                body(d)

            return carry

        lax.fori_loop(0, total, one, 0)

    for step in range(STEPS):
        buffer = step % 2
        if step:
            arrive(step - 1)

        def outer(n, carry):
            collide_slab(step, n * (width_x - 1))
            return carry

        lax.fori_loop(0, 2, outer, 0)
        for k in range(5):
            send_x[step, 0, k] = grid[buffer, PLUS_X[k], width_x, pl.ds(8, width_y), :]
            send_x[step, 1, k] = grid[buffer, MINUS_X[k], 1, pl.ds(8, width_y), :]
        for n, (i, step_x, step_y) in enumerate(CORNERS):
            x = width_x if step_x > 0 else 1
            row = width_y + 7 if step_y > 0 else 8
            line = grid[buffer, i, x, pl.ds(row, 1), :]
            send_c[step, n] = jnp.broadcast_to(line, (8, depth_z))
        if step == 0:
            pl.semaphore_wait(barrier, total - 1)
        for n in (0, 1, 4, 5, 6, 7):
            side(step, n).start()

        def inner(x, carry):
            collide_slab(step, x)
            return carry

        lax.fori_loop(1, width_x - 1, inner, 0)
        for k in range(5):
            for x in range(width_x):
                line = pl.ds(k * width_x + x, 1)
                send_y[step, 0, line, :] = grid[
                    buffer, PLUS_Y[k], x + 1, pl.ds(width_y + 7, 1), :
                ]
                send_y[step, 1, line, :] = grid[buffer, MINUS_Y[k], x + 1, pl.ds(8, 1), :]
        for n in (2, 3):
            side(step, n).start()
        sample(step)

    for_others(lambda d: panel_copy(d).start())
    own = pltpu.make_async_copy(payload.at[me_x], panels.at[me], own_sem)
    own.start()
    arrive(STEPS - 1)

    def final(x, carry):
        for tile in range(tiles_y):
            for i in range(19):
                out_ref[i, x, pl.ds(tile * 8, 8), :] = pulled((STEPS - 1) % 2, i, x, tile * 8)
        return carry

    lax.fori_loop(0, width_x, final, 0)
    own.wait()
    for_others(lambda d: panel_arrival(d).wait_recv())
    panels_ref[...] = panels[...]
    for_others(lambda d: panel_copy(d).wait_send())
    for step in range(STEPS):
        for n in range(8):
            side(step, n).wait_send()


SIN_POLY = (4.44288292, -7.30824569, 3.60635422, -0.84611165, 0.10982452)
COS_POLY = (1.4142135, -6.97885095, 5.73946038, -1.88355791, 0.31068803)


def horner(poly, x):
    value = poly[-1] * x + poly[-2]
    for coefficient in poly[-3::-1]:
        value = value * x + coefficient
    return value


def spectrum_table(freq_ref, lanes):
    shape = (STEPS * 8, lanes)
    row = lax.broadcasted_iota(jnp.int32, shape, 0)
    lane = lax.broadcasted_iota(jnp.int32, shape, 1)
    step, part, column, slot = row >> 3, row & 7, lane & 7, lane >> 3
    omega = jnp.zeros(shape, jnp.float32)
    for f in range(lanes // 8):
        omega = jnp.where(slot == f, freq_ref[0, f], omega)
    taper = jnp.zeros(shape, jnp.float32)
    for s in range(STEPS):
        taper = jnp.where(
            step == s, 0.5 - 0.5 * math.cos(2.0 * math.pi * (s + 0.5) / STEPS), taper
        )
    phase = omega * step.astype(jnp.float32)
    real, imag = taper * jnp.cos(phase), -taper * jnp.sin(phase)
    wave = omega * math.sqrt(3.0)
    vector = (part >= 1) & (part <= 3)
    table = jnp.where(vector & (column == part - 1), real * wave, 0.0)
    table = jnp.where(vector & (column == part + 2), imag * wave, table)
    table = jnp.where((part == 0) & (column == 6), real * omega, table)
    return jnp.where((part == 0) & (column == 7), imag * omega, table)


def green_kernel(
    capacity, count_ref, freq_ref, panels_ref, seen_ref, out_ref, sums, samples, amplitudes
):
    freqs = freq_ref.shape[1]
    sources = panels_ref.shape[0]
    observers = seen_ref.shape[1]
    sums[...] = jnp.zeros_like(sums)
    lane_of = lax.broadcasted_iota(jnp.int32, (capacity, 128), 1)

    live = 0
    for group in range(sources // 16):
        turned = panels_ref[pl.ds(group * 16, 16)].reshape(128, 128).T
        for n in range(16):
            piece = jnp.zeros((capacity, 128), jnp.float32)
            for step in range(STEPS):
                part = turned[step * capacity : (step + 1) * capacity]
                shift = (step * 8 - n * 8) % 128
                if shift:
                    part = pltpu.roll(part, shift, axis=1)
                piece = jnp.where((lane_of >> 3) == step, part, piece)
            samples[pl.ds(live, capacity), :] = piece
            live = live + count_ref[group * 16 + n]
    samples[pl.ds(live, 8), :] = jnp.zeros((8, 128), jnp.float32)

    table = spectrum_table(freq_ref, freqs * 8)

    def transform(n, carry):
        rows = pl.ds(pl.multiple_of(n * 128, 128), 128)
        amplitudes[rows, :] = jnp.dot(
            samples[rows, :][:, : STEPS * 8],
            table,
            precision=lax.Precision.HIGHEST,
            preferred_element_type=jnp.float32,
        )
        return carry

    lax.fori_loop(0, (live + 127) // 128, transform, 0)

    def tile(n, carry):
        rows = pl.ds(pl.multiple_of(n * 8, 8), 8)
        amplitude = amplitudes[rows, :]
        coords = samples[rows, :]
        offset = [seen_ref[pl.ds(a, 1), :] - coords[:, 4 + a : 5 + a] for a in range(3)]
        distance = jnp.sqrt(
            offset[0] * offset[0] + offset[1] * offset[1] + offset[2] * offset[2]
        )
        inverse = 1.0 / distance
        toward = [value * inverse for value in offset]
        for f in range(freqs):
            column = [
                jnp.broadcast_to(amplitude[:, f * 8 + c : f * 8 + c + 1], (8, observers))
                for c in range(8)
            ]
            turns = distance * freq_ref[1, f]
            turns = turns - jnp.round(turns)
            square = turns * turns
            half_sin = turns * horner(SIN_POLY, square)
            half_cos = horner(COS_POLY, square)
            cosine = 1.0 - half_sin * half_sin
            sine = half_sin * half_cos
            near = inverse * freq_ref[2, f]
            radial_re = toward[0] * column[0] + toward[1] * column[1] + toward[2] * column[2]
            radial_im = toward[0] * column[3] + toward[1] * column[4] + toward[2] * column[5]
            amp_re = radial_re * near - (radial_im + column[7])
            amp_im = radial_im * near + (radial_re + column[6])
            sums[2 * f] += inverse * (cosine * amp_re + sine * amp_im)
            sums[2 * f + 1] += inverse * (cosine * amp_im - sine * amp_re)
        return carry

    lax.fori_loop(0, (live + 7) // 8, tile, 0)
    for f in range(freqs):
        for part in range(2):
            out_ref[part, pl.ds(f, 1), :] = jnp.sum(sums[2 * f + part], axis=0, keepdims=True)


def local(
    populations, solid, panel_cell, panel_owner, panel_count, panel_area, observers, frequencies
):
    width_x, width_y, depth_z = solid.shape
    slots = panel_cell.shape[0]
    count_x, count_y = lax.axis_size("gx"), lax.axis_size("gy")
    total = count_x * count_y
    capacity = slots // count_x
    own_freq = frequencies.shape[0] // count_y
    brick_x, brick_y = lax.axis_index("gx"), lax.axis_index("gy")
    line = panel_cell // depth_z
    slot = jnp.arange(slots, dtype=jnp.int32)
    meta = jnp.stack(
        [
            panel_area[0],
            panel_area[1],
            panel_area[2],
            line.astype(jnp.float32),
            (brick_x * width_x + line // width_y).astype(jnp.float32),
            (brick_y * width_y + line % width_y).astype(jnp.float32),
            (panel_cell % depth_z).astype(jnp.float32),
            (slot < panel_count[0]).astype(jnp.float32),
        ]
    )
    earlier = (panel_owner[:, None] == panel_owner[None, :]) & (slot[:, None] < slot[None, :])
    position = panel_owner * capacity + jnp.sum(earlier.astype(jnp.int32), axis=0)
    meta = jnp.sum(
        jnp.where(position[None, :, None] == slot[None, None, :], meta[:, :, None], 0.0), axis=1
    )
    f32 = jnp.float32
    vmem = pl.BlockSpec(memory_space=pltpu.VMEM)
    smem = pl.BlockSpec(memory_space=pltpu.SMEM)
    rows_y = -(-5 * width_x // 8) * 8
    flow = pl.pallas_call(
        functools.partial(flow_kernel, count_x, count_y),
        out_shape=(
            jax.ShapeDtypeStruct(populations.shape, f32),
            jax.ShapeDtypeStruct((total, 8, 128), f32),
        ),
        in_specs=[vmem] * 3,
        out_specs=(vmem, vmem),
        scratch_shapes=[
            pltpu.VMEM((2, 19, width_x + 2, width_y + 16, depth_z), f32),
            pltpu.VMEM((4, width_x, width_y, depth_z), f32),
            pltpu.VMEM((STEPS, 2, 5, width_y, depth_z), f32),
            pltpu.VMEM((STEPS, 2, 5, width_y, depth_z), f32),
            pltpu.VMEM((STEPS, 2, rows_y, depth_z), f32),
            pltpu.VMEM((STEPS, 2, rows_y, depth_z), f32),
            pltpu.VMEM((STEPS, 4, 8, depth_z), f32),
            pltpu.VMEM((STEPS, 4, 8, depth_z), f32),
            pltpu.VMEM((count_x, 8, 128), f32),
            pltpu.VMEM((total, 8, 128), f32),
            pltpu.SemaphoreType.DMA((STEPS, 8)),
            pltpu.SemaphoreType.DMA((STEPS, 8)),
            pltpu.SemaphoreType.DMA((total,)),
            pltpu.SemaphoreType.DMA((total,)),
            pltpu.SemaphoreType.DMA,
        ],
        compiler_params=pltpu.CompilerParams(
            collective_id=0, has_side_effects=True, vmem_limit_bytes=40 * 1024 * 1024
        ),
        name="flow",
    )
    current, panels = flow(populations, solid, meta)

    own_list = lax.dynamic_slice_in_dim(frequencies, brick_y * own_freq, own_freq)
    wave = own_list * math.sqrt(3.0)
    tones = jnp.stack([own_list, wave * (0.5 / math.pi), 1.0 / wave])
    live_in = jnp.sum(panels[:, 7, :capacity], axis=1).astype(jnp.int32)
    room = (-(-(total * capacity) // 128) + 1) * 128
    spectra = pl.pallas_call(
        functools.partial(green_kernel, capacity),
        out_shape=jax.ShapeDtypeStruct((2, own_freq, observers.shape[1]), f32),
        in_specs=[smem] * 2 + [vmem] * 2,
        out_specs=vmem,
        scratch_shapes=[
            pltpu.VMEM((2 * own_freq, 8, observers.shape[1]), f32),
            pltpu.VMEM((room, 128), f32),
            pltpu.VMEM((room, own_freq * 8), f32),
        ],
        compiler_params=pltpu.CompilerParams(vmem_limit_bytes=40 * 1024 * 1024),
        name="green",
    )(live_in, tones, panels, observers)
    return (current, spectra[None])


def solution(mesh):
    return jax.shard_map(
        local,
        mesh=mesh,
        in_specs=(
            P(None, "gx", "gy", None),
            P("gx", "gy", None),
            P(("gx", "gy")),
            P(("gx", "gy")),
            P(("gx", "gy")),
            P(None, ("gx", "gy")),
            P(),
            P(),
        ),
        out_specs=(P(None, "gx", "gy", None), P("gx", None, "gy", None)),
        check_vma=False,
    )
```

```python
import functools
import math

import jax
import jax.numpy as jnp
import numpy as np
from jax import lax
from jax.experimental import pallas as pl
from jax.experimental.pallas import tpu as pltpu
from jax.sharding import PartitionSpec as P

STEPS = 4


VELOCITIES = np.array(
    [
        [0, 0, 0],
        [1, 0, 0],
        [-1, 0, 0],
        [0, 1, 0],
        [0, -1, 0],
        [0, 0, 1],
        [0, 0, -1],
        [1, 1, 0],
        [-1, -1, 0],
        [1, -1, 0],
        [-1, 1, 0],
        [1, 0, 1],
        [-1, 0, -1],
        [1, 0, -1],
        [-1, 0, 1],
        [0, 1, 1],
        [0, -1, -1],
        [0, 1, -1],
        [0, -1, 1],
    ]
)
OPPOSITE = [0, 2, 1, 4, 3, 6, 5, 8, 7, 10, 9, 12, 11, 14, 13, 16, 15, 18, 17]
LATTICE_WEIGHTS = [1.0 / 3.0] + [1.0 / 18.0] * 6 + [1.0 / 36.0] * 12


def moment_basis():
    along_x = VELOCITIES[:, 0]
    along_y = VELOCITIES[:, 1]
    along_z = VELOCITIES[:, 2]
    constant = np.ones(19)
    raw_list = [
        constant,
        along_x,
        along_y,
        along_z,
        along_x * along_x,
        along_y * along_y,
        along_z * along_z,
        along_x * along_y,
        along_x * along_z,
        along_y * along_z,
        along_x * along_x * along_y,
        along_x * along_x * along_z,
        along_y * along_y * along_x,
        along_y * along_y * along_z,
        along_z * along_z * along_x,
        along_z * along_z * along_y,
        along_x * along_x * along_y * along_y,
        along_x * along_x * along_z * along_z,
        along_y * along_y * along_z * along_z,
    ]
    basis = []
    for vector in raw_list:
        column = np.array(vector) * 1.0
        for previous in basis:
            column = column - previous * (column @ previous) / (previous @ previous)
        basis.append(column)
    matrix = np.stack(basis)
    return matrix


PAIRS = [1, 3, 5, 7, 9, 11, 13, 15, 17]
PLUS_X = [i for i in range(19) if VELOCITIES[i][0] == 1]
MINUS_X = [i for i in range(19) if VELOCITIES[i][0] == -1]
PLUS_Y = [i for i in range(19) if VELOCITIES[i][1] == 1]
MINUS_Y = [i for i in range(19) if VELOCITIES[i][1] == -1]
CORNERS = [(7, 1, 1), (8, -1, -1), (9, 1, -1), (10, -1, 1)]
CLASS_OF_PAIR = [1, 2, 3, 4, 4, 5, 5, 6, 6]
CLASS_MEMBER = [0, 1, 3, 5, 7, 11, 15]
MOMENTS = moment_basis()
MESH = pl.DeviceIdType.MESH


def signed_sum(terms):
    total = None
    for sign, value in terms:
        if total is None:
            total = value if sign > 0 else -value
        else:
            total = total + value if sign > 0 else total - value
    return total


def along(axis, odd):
    return signed_sum(
        [
            (VELOCITIES[i][axis], odd[n])
            for n, i in enumerate(PAIRS)
            if VELOCITIES[i][axis] != 0
        ]
    )


def tree_sum(values):
    values = list(values)
    while len(values) > 1:
        values = [
            values[i] + values[i + 1] if i + 1 < len(values) else values[i]
            for i in range(0, len(values), 2)
        ]
    return values[0]


def collide_tile(f, solid):
    even = [f[i] + f[i + 1] for i in PAIRS]
    odd = [f[i] - f[i + 1] for i in PAIRS]
    rho = tree_sum([f[0]] + even)
    inverse = 1.0 / rho
    u = [along(axis, odd) * inverse for axis in range(3)]
    base = 1.0 - 1.5 * (u[0] * u[0] + u[1] * u[1] + u[2] * u[2])
    scaled = {w: rho * w for w in (1.0 / 9.0, 1.0 / 18.0)}
    rest = f[0] - (rho * (1.0 / 3.0)) * base
    d_even, d_odd = [], []
    for n, i in enumerate(PAIRS):
        weight = scaled[1.0 / 9.0] if i < 7 else scaled[1.0 / 18.0]
        cu = signed_sum([(VELOCITIES[i][a], u[a]) for a in range(3) if VELOCITIES[i][a] != 0])
        d_even.append(even[n] - weight * (base + 4.5 * (cu * cu)))
        d_odd.append(odd[n] - weight * (3.0 * cu))
    mean = tree_sum([rest] + d_even) * (1.8 / 19.0)
    drift = [along(axis, d_odd) * (1.4 / 10.0) for axis in range(3)]
    classes = [rest] + [
        tree_sum([d_even[n] for n in range(9) if CLASS_OF_PAIR[n] == c]) for c in range(1, 7)
    ]
    high = [mean] * 7
    for k in range(16, 19):
        row = MOMENTS[k]
        norm = float(row @ row)
        picked = [(c, float(row[m])) for c, m in enumerate(CLASS_MEMBER) if abs(row[m]) > 1e-9]
        moment = tree_sum([classes[c] * value for c, value in picked])
        for c, value in picked:
            high[c] = high[c] + moment * (0.6 * value / norm)
    relaxed = [None] * 19
    relaxed[0] = f[0] - (1.8 * rest - high[0])
    for n, i in enumerate(PAIRS):
        part_e = 0.9 * d_even[n] - high[CLASS_OF_PAIR[n]]
        part_o = 0.7 * d_odd[n] - signed_sum(
            [(VELOCITIES[i][a], drift[a]) for a in range(3) if VELOCITIES[i][a] != 0]
        )
        relaxed[i] = jnp.where(solid, f[i + 1], f[i] - (part_e + part_o))
        relaxed[i + 1] = jnp.where(solid, f[i], f[i + 1] - (part_e - part_o))
    relaxed[0] = jnp.where(solid, f[0], relaxed[0])
    return relaxed, rho, u


def flow_kernel(
    count_x,
    count_y,
    source_ref,
    walls_ref,
    listed_ref,
    out_ref,
    panels_ref,
    f_ref,
    solid_ref,
    meta_ref,
    in_sem,
    grid,
    fields,
    send_x,
    recv_x,
    send_y,
    recv_y,
    send_c,
    recv_c,
    payload,
    panels,
    step_send,
    step_recv,
    panel_send,
    panel_recv,
    own_sem,
):
    width_x, width_y, depth_z = solid_ref.shape
    slots = meta_ref.shape[1]
    capacity = slots // count_x
    total = count_x * count_y
    me_x, me_y = lax.axis_index("gx"), lax.axis_index("gy")
    me = me_x * count_y + me_y
    tiles_y = width_y // 8

    loads = [
        pltpu.make_async_copy(source_ref.at[:, x], f_ref.at[:, x], in_sem.at[x])
        for x in range(width_x)
    ]
    walls = pltpu.make_async_copy(walls_ref, solid_ref, in_sem.at[width_x])
    walls.start()
    for x in [0, width_x - 1] + list(range(1, width_x - 1)):
        loads[x].start()

    barrier = pltpu.get_barrier_semaphore()

    def greet(d, carry):
        @pl.when(d != me)
        def _():
            pl.semaphore_signal(
                barrier,
                inc=1,
                device_id=(d // count_y, d % count_y),
                device_id_type=MESH,
            )

        return carry

    lax.fori_loop(0, total, greet, 0)

    right_x, left_x = lax.rem(me_x + 1, count_x), lax.rem(me_x + count_x - 1, count_x)
    right_y, left_y = lax.rem(me_y + 1, count_y), lax.rem(me_y + count_y - 1, count_y)

    def side(step, n):
        if n < 2:
            source, target = send_x.at[step, n], recv_x.at[step, n]
            place = (right_x if n == 0 else left_x, me_y)
        elif n < 4:
            source, target = send_y.at[step, n - 2], recv_y.at[step, n - 2]
            place = (me_x, right_y if n == 2 else left_y)
        else:
            _, step_x, step_y = CORNERS[n - 4]
            source, target = send_c.at[step, n - 4], recv_c.at[step, n - 4]
            place = (right_x if step_x > 0 else left_x, right_y if step_y > 0 else left_y)
        return pltpu.make_async_remote_copy(
            src_ref=source,
            dst_ref=target,
            send_sem=step_send.at[step, n],
            recv_sem=step_recv.at[step, n],
            device_id=place,
            device_id_type=MESH,
        )

    def pulled(buffer, i, x, row):
        step_x, step_y, step_z = (int(v) for v in VELOCITIES[i])
        value = grid[buffer, i, x + 1 - step_x, pl.ds(row + 8 - step_y, 8), :]
        if step_z:
            value = pltpu.roll(value, step_z % depth_z, axis=1)
        return value

    def collide_slab(step, x):
        for tile in range(tiles_y):
            row = tile * 8
            if step == 0:
                f = [f_ref[i, x, pl.ds(row, 8), :] for i in range(19)]
            else:
                f = [pulled((step - 1) % 2, i, x, row) for i in range(19)]
            relaxed, rho, u = collide_tile(f, solid_ref[x, pl.ds(row, 8), :] > 0)
            for i in range(19):
                grid[step % 2, i, x + 1, pl.ds(row + 8, 8), :] = relaxed[i]
            for n, value in enumerate([rho] + u):
                fields[n, x, pl.ds(row, 8), :] = value

    def arrive(step):
        buffer = step % 2
        for n in range(8):
            side(step, n).wait_recv()
        for k in range(5):
            grid[buffer, PLUS_X[k], 0, pl.ds(8, width_y), :] = recv_x[step, 0, k]
            grid[buffer, MINUS_X[k], width_x + 1, pl.ds(8, width_y), :] = recv_x[step, 1, k]
        for k in range(5):
            for x in range(width_x):
                line = pl.ds(k * width_x + x, 1)
                grid[buffer, PLUS_Y[k], x + 1, pl.ds(7, 1), :] = recv_y[step, 0, line, :]
                grid[buffer, MINUS_Y[k], x + 1, pl.ds(width_y + 8, 1), :] = recv_y[step, 1, line, :]
        for n, (i, step_x, step_y) in enumerate(CORNERS):
            x = 0 if step_x > 0 else width_x + 1
            row = 7 if step_y > 0 else width_y + 8
            grid[buffer, i, x, pl.ds(row, 1), :] = recv_c[step, n, pl.ds(0, 1), :]

    def sort_panels():
        owner = jnp.broadcast_to(listed_ref[pl.ds(8, 1), :], (slots, slots))
        first = lax.broadcasted_iota(jnp.int32, (slots, slots), 0).astype(jnp.float32)
        second = lax.broadcasted_iota(jnp.int32, (slots, slots), 1).astype(jnp.float32)
        earlier = (owner.T == owner) & (first < second)
        rank = jnp.sum(jnp.where(earlier, 1.0, 0.0), axis=0, keepdims=True)
        position = jnp.broadcast_to(
            listed_ref[pl.ds(8, 1), :] * float(capacity) + rank, (slots, slots)
        )
        moved = jnp.where(position.T == second, 1.0, 0.0)
        meta_ref[...] = jnp.dot(
            listed_ref[pl.ds(0, 8), :],
            moved,
            precision=lax.Precision.HIGHEST,
            preferred_element_type=jnp.float32,
        )

    cells = lax.broadcasted_iota(jnp.int32, (depth_z, slots), 0).astype(jnp.float32)
    lines = lax.broadcasted_iota(jnp.int32, (width_x * width_y, slots), 0).astype(jnp.float32)
    row_of = lax.broadcasted_iota(jnp.int32, (8, slots), 0)
    lane_of = lax.broadcasted_iota(jnp.int32, (8, 128), 1)

    def sample(step):
        at_z = jnp.where(cells == meta_ref[pl.ds(6, 1), :], 1.0, 0.0).astype(jnp.bfloat16)
        data = fields[...].reshape(4 * width_x * width_y, depth_z)
        high = data.astype(jnp.bfloat16)
        left = data - high.astype(jnp.float32)
        middle = left.astype(jnp.bfloat16)
        low = (left - middle.astype(jnp.float32)).astype(jnp.bfloat16)
        picked = sum(
            jnp.dot(part, at_z, preferred_element_type=jnp.float32) for part in (high, middle, low)
        )
        at_line = lines == meta_ref[pl.ds(3, 1), :]
        count = width_x * width_y
        rho, ux, uy, uz = (
            jnp.sum(
                jnp.where(at_line, picked[n * count : (n + 1) * count], 0.0), axis=0, keepdims=True
            )
            for n in range(4)
        )
        area = [meta_ref[pl.ds(a, 1), :] for a in range(3)]
        live = meta_ref[pl.ds(7, 1), :]
        flux = ux * area[0] + uy * area[1] + uz * area[2]
        terms = [rho * flux] + [
            (rho - 19.0) / 3.0 * a + rho * v * flux for a, v in zip(area, (ux, uy, uz))
        ]
        block = meta_ref[...] if step == 0 else jnp.zeros((8, slots), jnp.float32)
        for n in range(4):
            block = jnp.where(row_of == n, terms[n] * live, block)
        for q in range(count_x):
            start = q * capacity
            part = block[:, start // 128 * 128 : start // 128 * 128 + 128]
            shift = (step * capacity - start) % 128
            if shift:
                part = pltpu.roll(part, shift, axis=1)
            here = (lane_of >= step * capacity) & (lane_of < (step + 1) * capacity)
            old = payload[q] if step else jnp.zeros((8, 128), jnp.float32)
            payload[q] = jnp.where(here, part, old)

    def panel_copy(d):
        return pltpu.make_async_remote_copy(
            src_ref=payload.at[d // count_y],
            dst_ref=panels.at[me],
            send_sem=panel_send.at[d],
            recv_sem=panel_recv.at[me],
            device_id=(d // count_y, d % count_y),
            device_id_type=MESH,
        )

    def panel_arrival(d):
        return pltpu.make_async_remote_copy(
            src_ref=payload.at[d // count_y],
            dst_ref=panels.at[d],
            send_sem=panel_send.at[d],
            recv_sem=panel_recv.at[d],
            device_id=(d // count_y, d % count_y),
            device_id_type=MESH,
        )

    def for_others(body):
        def one(d, carry):
            @pl.when(d != me)
            def _():
                body(d)

            return carry

        lax.fori_loop(0, total, one, 0)

    for step in range(STEPS):
        buffer = step % 2
        if step:
            arrive(step - 1)
        else:
            walls.wait()
            loads[0].wait()
            loads[width_x - 1].wait()

        def outer(n, carry):
            collide_slab(step, n * (width_x - 1))
            return carry

        lax.fori_loop(0, 2, outer, 0)
        for k in range(5):
            send_x[step, 0, k] = grid[buffer, PLUS_X[k], width_x, pl.ds(8, width_y), :]
            send_x[step, 1, k] = grid[buffer, MINUS_X[k], 1, pl.ds(8, width_y), :]
        for n, (i, step_x, step_y) in enumerate(CORNERS):
            x = width_x if step_x > 0 else 1
            row = width_y + 7 if step_y > 0 else 8
            line = grid[buffer, i, x, pl.ds(row, 1), :]
            send_c[step, n] = jnp.broadcast_to(line, (8, depth_z))
        if step == 0:
            pl.semaphore_wait(barrier, total - 1)
        for n in (0, 1, 4, 5, 6, 7):
            side(step, n).start()

        if step == 0:
            for x in range(1, width_x - 1):
                loads[x].wait()

        def inner(x, carry):
            collide_slab(step, x)
            return carry

        lax.fori_loop(1, width_x - 1, inner, 0)
        for k in range(5):
            for x in range(width_x):
                line = pl.ds(k * width_x + x, 1)
                send_y[step, 0, line, :] = grid[
                    buffer, PLUS_Y[k], x + 1, pl.ds(width_y + 7, 1), :
                ]
                send_y[step, 1, line, :] = grid[buffer, MINUS_Y[k], x + 1, pl.ds(8, 1), :]
        for n in (2, 3):
            side(step, n).start()
        if step == 0:
            sort_panels()
        sample(step)

    for_others(lambda d: panel_copy(d).start())
    own = pltpu.make_async_copy(payload.at[me_x], panels.at[me], own_sem)
    own.start()
    arrive(STEPS - 1)

    def final(x, carry):
        for tile in range(tiles_y):
            for i in range(19):
                out_ref[i, x, pl.ds(tile * 8, 8), :] = pulled((STEPS - 1) % 2, i, x, tile * 8)
        return carry

    lax.fori_loop(0, width_x, final, 0)
    own.wait()
    for_others(lambda d: panel_arrival(d).wait_recv())
    panels_ref[...] = panels[...]
    for_others(lambda d: panel_copy(d).wait_send())
    for step in range(STEPS):
        for n in range(8):
            side(step, n).wait_send()


SIN_POLY = (4.44288292, -7.30824569, 3.60635422, -0.84611165, 0.10982452)
COS_POLY = (1.4142135, -6.97885095, 5.73946038, -1.88355791, 0.31068803)


def horner(poly, x):
    value = poly[-1] * x + poly[-2]
    for coefficient in poly[-3::-1]:
        value = value * x + coefficient
    return value


def spectrum_table(freq_ref, lanes):
    shape = (STEPS * 8, lanes)
    row = lax.broadcasted_iota(jnp.int32, shape, 0)
    lane = lax.broadcasted_iota(jnp.int32, shape, 1)
    step, part, column, slot = row >> 3, row & 7, lane & 7, lane >> 3
    omega = jnp.zeros(shape, jnp.float32)
    for f in range(lanes // 8):
        omega = jnp.where(slot == f, freq_ref[0, f], omega)
    taper = jnp.zeros(shape, jnp.float32)
    for s in range(STEPS):
        taper = jnp.where(
            step == s, 0.5 - 0.5 * math.cos(2.0 * math.pi * (s + 0.5) / STEPS), taper
        )
    phase = omega * step.astype(jnp.float32)
    real, imag = taper * jnp.cos(phase), -taper * jnp.sin(phase)
    wave = omega * math.sqrt(3.0)
    vector = (part >= 1) & (part <= 3)
    table = jnp.where(vector & (column == part - 1), real * wave, 0.0)
    table = jnp.where(vector & (column == part + 2), imag * wave, table)
    table = jnp.where((part == 0) & (column == 6), real * omega, table)
    return jnp.where((part == 0) & (column == 7), imag * omega, table)


def green_kernel(
    capacity, count_ref, freq_ref, panels_ref, seen_ref, out_ref, sums, samples, amplitudes
):
    freqs = freq_ref.shape[1]
    sources = panels_ref.shape[0]
    observers = seen_ref.shape[1]
    sums[...] = jnp.zeros_like(sums)
    lane_of = lax.broadcasted_iota(jnp.int32, (capacity, 128), 1)

    live = 0
    for group in range(sources // 16):
        turned = panels_ref[pl.ds(group * 16, 16)].reshape(128, 128).T
        for n in range(16):
            piece = jnp.zeros((capacity, 128), jnp.float32)
            for step in range(STEPS):
                part = turned[step * capacity : (step + 1) * capacity]
                shift = (step * 8 - n * 8) % 128
                if shift:
                    part = pltpu.roll(part, shift, axis=1)
                piece = jnp.where((lane_of >> 3) == step, part, piece)
            samples[pl.ds(live, capacity), :] = piece
            live = live + count_ref[group * 16 + n]
    samples[pl.ds(live, 8), :] = jnp.zeros((8, 128), jnp.float32)

    table = spectrum_table(freq_ref, freqs * 8)

    def transform(n, carry):
        rows = pl.ds(pl.multiple_of(n * 128, 128), 128)
        amplitudes[rows, :] = jnp.dot(
            samples[rows, :][:, : STEPS * 8],
            table,
            precision=lax.Precision.HIGHEST,
            preferred_element_type=jnp.float32,
        )
        return carry

    lax.fori_loop(0, (live + 127) // 128, transform, 0)

    def tile(n, carry):
        rows = pl.ds(pl.multiple_of(n * 8, 8), 8)
        amplitude = amplitudes[rows, :]
        coords = samples[rows, :]
        offset = [seen_ref[pl.ds(a, 1), :] - coords[:, 4 + a : 5 + a] for a in range(3)]
        distance = jnp.sqrt(
            offset[0] * offset[0] + offset[1] * offset[1] + offset[2] * offset[2]
        )
        inverse = 1.0 / distance
        toward = [value * inverse for value in offset]
        for f in range(freqs):
            column = [
                jnp.broadcast_to(amplitude[:, f * 8 + c : f * 8 + c + 1], (8, observers))
                for c in range(8)
            ]
            turns = distance * freq_ref[1, f]
            turns = turns - jnp.round(turns)
            square = turns * turns
            half_sin = turns * horner(SIN_POLY, square)
            half_cos = horner(COS_POLY, square)
            cosine = 1.0 - half_sin * half_sin
            sine = half_sin * half_cos
            near = inverse * freq_ref[2, f]
            radial_re = toward[0] * column[0] + toward[1] * column[1] + toward[2] * column[2]
            radial_im = toward[0] * column[3] + toward[1] * column[4] + toward[2] * column[5]
            amp_re = radial_re * near - (radial_im + column[7])
            amp_im = radial_im * near + (radial_re + column[6])
            sums[2 * f] += inverse * (cosine * amp_re + sine * amp_im)
            sums[2 * f + 1] += inverse * (cosine * amp_im - sine * amp_re)
        return carry

    lax.fori_loop(0, (live + 7) // 8, tile, 0)
    for f in range(freqs):
        for part in range(2):
            out_ref[part, pl.ds(f, 1), :] = jnp.sum(sums[2 * f + part], axis=0, keepdims=True)


def local(
    populations, solid, panel_cell, panel_owner, panel_count, panel_area, observers, frequencies
):
    width_x, width_y, depth_z = solid.shape
    slots = panel_cell.shape[0]
    count_x, count_y = lax.axis_size("gx"), lax.axis_size("gy")
    total = count_x * count_y
    capacity = slots // count_x
    own_freq = frequencies.shape[0] // count_y
    brick_x, brick_y = lax.axis_index("gx"), lax.axis_index("gy")
    line = panel_cell // depth_z
    slot = jnp.arange(slots, dtype=jnp.int32)
    meta = jnp.stack(
        [
            panel_area[0],
            panel_area[1],
            panel_area[2],
            line.astype(jnp.float32),
            (brick_x * width_x + line // width_y).astype(jnp.float32),
            (brick_y * width_y + line % width_y).astype(jnp.float32),
            (panel_cell % depth_z).astype(jnp.float32),
            (slot < panel_count[0]).astype(jnp.float32),
        ]
        + [panel_owner.astype(jnp.float32)] * 8
    )
    f32 = jnp.float32
    vmem = pl.BlockSpec(memory_space=pltpu.VMEM)
    smem = pl.BlockSpec(memory_space=pltpu.SMEM)
    rows_y = -(-5 * width_x // 8) * 8
    flow = pl.pallas_call(
        functools.partial(flow_kernel, count_x, count_y),
        out_shape=(
            jax.ShapeDtypeStruct(populations.shape, f32),
            jax.ShapeDtypeStruct((total, 8, 128), f32),
        ),
        in_specs=[pl.BlockSpec(memory_space=pltpu.HBM)] * 2 + [vmem],
        out_specs=(vmem, vmem),
        scratch_shapes=[
            pltpu.VMEM(populations.shape, f32),
            pltpu.VMEM(solid.shape, solid.dtype),
            pltpu.VMEM((8, slots), f32),
            pltpu.SemaphoreType.DMA((width_x + 1,)),
            pltpu.VMEM((2, 19, width_x + 2, width_y + 16, depth_z), f32),
            pltpu.VMEM((4, width_x, width_y, depth_z), f32),
            pltpu.VMEM((STEPS, 2, 5, width_y, depth_z), f32),
            pltpu.VMEM((STEPS, 2, 5, width_y, depth_z), f32),
            pltpu.VMEM((STEPS, 2, rows_y, depth_z), f32),
            pltpu.VMEM((STEPS, 2, rows_y, depth_z), f32),
            pltpu.VMEM((STEPS, 4, 8, depth_z), f32),
            pltpu.VMEM((STEPS, 4, 8, depth_z), f32),
            pltpu.VMEM((count_x, 8, 128), f32),
            pltpu.VMEM((total, 8, 128), f32),
            pltpu.SemaphoreType.DMA((STEPS, 8)),
            pltpu.SemaphoreType.DMA((STEPS, 8)),
            pltpu.SemaphoreType.DMA((total,)),
            pltpu.SemaphoreType.DMA((total,)),
            pltpu.SemaphoreType.DMA,
        ],
        compiler_params=pltpu.CompilerParams(
            collective_id=0, has_side_effects=True, vmem_limit_bytes=40 * 1024 * 1024
        ),
        name="flow",
    )
    current, panels = flow(populations, solid, meta)

    own_list = lax.dynamic_slice_in_dim(frequencies, brick_y * own_freq, own_freq)
    wave = own_list * math.sqrt(3.0)
    tones = jnp.stack([own_list, wave * (0.5 / math.pi), 1.0 / wave])
    live_in = jnp.sum(panels[:, 7, :capacity], axis=1).astype(jnp.int32)
    room = (-(-(total * capacity) // 128) + 1) * 128
    spectra = pl.pallas_call(
        functools.partial(green_kernel, capacity),
        out_shape=jax.ShapeDtypeStruct((2, own_freq, observers.shape[1]), f32),
        in_specs=[smem] * 2 + [vmem] * 2,
        out_specs=vmem,
        scratch_shapes=[
            pltpu.VMEM((2 * own_freq, 8, observers.shape[1]), f32),
            pltpu.VMEM((room, 128), f32),
            pltpu.VMEM((room, own_freq * 8), f32),
        ],
        compiler_params=pltpu.CompilerParams(vmem_limit_bytes=40 * 1024 * 1024),
        name="green",
    )(live_in, tones, panels, observers)
    return (current, spectra[None])


def solution(mesh):
    return jax.shard_map(
        local,
        mesh=mesh,
        in_specs=(
            P(None, "gx", "gy", None),
            P("gx", "gy", None),
            P(("gx", "gy")),
            P(("gx", "gy")),
            P(("gx", "gy")),
            P(None, ("gx", "gy")),
            P(),
            P(),
        ),
        out_specs=(P(None, "gx", "gy", None), P("gx", None, "gy", None)),
        check_vma=False,
    )
```

```python
import functools
import math

import jax
import jax.numpy as jnp
import numpy as np
from jax import lax
from jax.experimental import pallas as pl
from jax.experimental.pallas import tpu as pltpu
from jax.sharding import PartitionSpec as P

STEPS = 4


VELOCITIES = np.array(
    [
        [0, 0, 0],
        [1, 0, 0],
        [-1, 0, 0],
        [0, 1, 0],
        [0, -1, 0],
        [0, 0, 1],
        [0, 0, -1],
        [1, 1, 0],
        [-1, -1, 0],
        [1, -1, 0],
        [-1, 1, 0],
        [1, 0, 1],
        [-1, 0, -1],
        [1, 0, -1],
        [-1, 0, 1],
        [0, 1, 1],
        [0, -1, -1],
        [0, 1, -1],
        [0, -1, 1],
    ]
)
OPPOSITE = [0, 2, 1, 4, 3, 6, 5, 8, 7, 10, 9, 12, 11, 14, 13, 16, 15, 18, 17]
LATTICE_WEIGHTS = [1.0 / 3.0] + [1.0 / 18.0] * 6 + [1.0 / 36.0] * 12


def moment_basis():
    along_x = VELOCITIES[:, 0]
    along_y = VELOCITIES[:, 1]
    along_z = VELOCITIES[:, 2]
    constant = np.ones(19)
    raw_list = [
        constant,
        along_x,
        along_y,
        along_z,
        along_x * along_x,
        along_y * along_y,
        along_z * along_z,
        along_x * along_y,
        along_x * along_z,
        along_y * along_z,
        along_x * along_x * along_y,
        along_x * along_x * along_z,
        along_y * along_y * along_x,
        along_y * along_y * along_z,
        along_z * along_z * along_x,
        along_z * along_z * along_y,
        along_x * along_x * along_y * along_y,
        along_x * along_x * along_z * along_z,
        along_y * along_y * along_z * along_z,
    ]
    basis = []
    for vector in raw_list:
        column = np.array(vector) * 1.0
        for previous in basis:
            column = column - previous * (column @ previous) / (previous @ previous)
        basis.append(column)
    matrix = np.stack(basis)
    return matrix


PAIRS = [1, 3, 5, 7, 9, 11, 13, 15, 17]
PLUS_X = [i for i in range(19) if VELOCITIES[i][0] == 1]
MINUS_X = [i for i in range(19) if VELOCITIES[i][0] == -1]
PLUS_Y = [i for i in range(19) if VELOCITIES[i][1] == 1]
MINUS_Y = [i for i in range(19) if VELOCITIES[i][1] == -1]
CORNERS = [(7, 1, 1), (8, -1, -1), (9, 1, -1), (10, -1, 1)]
CLASS_OF_PAIR = [1, 2, 3, 4, 4, 5, 5, 6, 6]
CLASS_MEMBER = [0, 1, 3, 5, 7, 11, 15]
MOMENTS = moment_basis()
MESH = pl.DeviceIdType.MESH


def signed_sum(terms):
    total = None
    for sign, value in terms:
        if total is None:
            total = value if sign > 0 else -value
        else:
            total = total + value if sign > 0 else total - value
    return total


def along(axis, odd):
    return signed_sum(
        [
            (VELOCITIES[i][axis], odd[n])
            for n, i in enumerate(PAIRS)
            if VELOCITIES[i][axis] != 0
        ]
    )


def tree_sum(values):
    values = list(values)
    while len(values) > 1:
        values = [
            values[i] + values[i + 1] if i + 1 < len(values) else values[i]
            for i in range(0, len(values), 2)
        ]
    return values[0]


def collide_tile(f, solid):
    even = [f[i] + f[i + 1] for i in PAIRS]
    odd = [f[i] - f[i + 1] for i in PAIRS]
    rho = tree_sum([f[0]] + even)
    inverse = 1.0 / rho
    u = [along(axis, odd) * inverse for axis in range(3)]
    base = 1.0 - 1.5 * (u[0] * u[0] + u[1] * u[1] + u[2] * u[2])
    scaled = {w: rho * w for w in (1.0 / 9.0, 1.0 / 18.0)}
    rest = f[0] - (rho * (1.0 / 3.0)) * base
    d_even, d_odd = [], []
    for n, i in enumerate(PAIRS):
        weight = scaled[1.0 / 9.0] if i < 7 else scaled[1.0 / 18.0]
        cu = signed_sum([(VELOCITIES[i][a], u[a]) for a in range(3) if VELOCITIES[i][a] != 0])
        d_even.append(even[n] - weight * (base + 4.5 * (cu * cu)))
        d_odd.append(odd[n] - weight * (3.0 * cu))
    mean = tree_sum([rest] + d_even) * (1.8 / 19.0)
    drift = [along(axis, d_odd) * (1.4 / 10.0) for axis in range(3)]
    classes = [rest] + [
        tree_sum([d_even[n] for n in range(9) if CLASS_OF_PAIR[n] == c]) for c in range(1, 7)
    ]
    high = [mean] * 7
    for k in range(16, 19):
        row = MOMENTS[k]
        norm = float(row @ row)
        picked = [(c, float(row[m])) for c, m in enumerate(CLASS_MEMBER) if abs(row[m]) > 1e-9]
        moment = tree_sum([classes[c] * value for c, value in picked])
        for c, value in picked:
            high[c] = high[c] + moment * (0.6 * value / norm)
    relaxed = [None] * 19
    relaxed[0] = f[0] - (1.8 * rest - high[0])
    for n, i in enumerate(PAIRS):
        part_e = 0.9 * d_even[n] - high[CLASS_OF_PAIR[n]]
        part_o = 0.7 * d_odd[n] - signed_sum(
            [(VELOCITIES[i][a], drift[a]) for a in range(3) if VELOCITIES[i][a] != 0]
        )
        relaxed[i] = jnp.where(solid, f[i + 1], f[i] - (part_e + part_o))
        relaxed[i + 1] = jnp.where(solid, f[i], f[i + 1] - (part_e - part_o))
    relaxed[0] = jnp.where(solid, f[0], relaxed[0])
    return relaxed, rho, u


def flow_kernel(
    count_x,
    count_y,
    source_ref,
    walls_ref,
    listed_ref,
    out_ref,
    panels_ref,
    f_ref,
    solid_ref,
    meta_ref,
    in_sem,
    grid,
    fields,
    send_x,
    recv_x,
    send_y,
    recv_y,
    send_c,
    recv_c,
    payload,
    panels,
    step_send,
    step_recv,
    panel_send,
    panel_recv,
    own_sem,
):
    width_x, width_y, depth_z = solid_ref.shape
    slots = meta_ref.shape[1]
    capacity = slots // count_x
    total = count_x * count_y
    me_x, me_y = lax.axis_index("gx"), lax.axis_index("gy")
    me = me_x * count_y + me_y
    tiles_y = width_y // 8

    loads = [
        pltpu.make_async_copy(source_ref.at[:, x], f_ref.at[:, x], in_sem.at[x])
        for x in range(width_x)
    ]
    walls = pltpu.make_async_copy(walls_ref, solid_ref, in_sem.at[width_x])
    walls.start()
    for x in [0, width_x - 1] + list(range(1, width_x - 1)):
        loads[x].start()

    barrier = pltpu.get_barrier_semaphore()

    def greet(d, carry):
        @pl.when(d != me)
        def _():
            pl.semaphore_signal(
                barrier,
                inc=1,
                device_id=(d // count_y, d % count_y),
                device_id_type=MESH,
            )

        return carry

    lax.fori_loop(0, total, greet, 0)

    right_x, left_x = lax.rem(me_x + 1, count_x), lax.rem(me_x + count_x - 1, count_x)
    right_y, left_y = lax.rem(me_y + 1, count_y), lax.rem(me_y + count_y - 1, count_y)

    def side(step, n):
        if n < 2:
            source, target = send_x.at[step, n], recv_x.at[step, n]
            place = (right_x if n == 0 else left_x, me_y)
        elif n < 4:
            source, target = send_y.at[step, n - 2], recv_y.at[step, n - 2]
            place = (me_x, right_y if n == 2 else left_y)
        else:
            _, step_x, step_y = CORNERS[n - 4]
            source, target = send_c.at[step, n - 4], recv_c.at[step, n - 4]
            place = (right_x if step_x > 0 else left_x, right_y if step_y > 0 else left_y)
        return pltpu.make_async_remote_copy(
            src_ref=source,
            dst_ref=target,
            send_sem=step_send.at[step, n],
            recv_sem=step_recv.at[step, n],
            device_id=place,
            device_id_type=MESH,
        )

    def pulled(buffer, i, x, row):
        step_x, step_y, step_z = (int(v) for v in VELOCITIES[i])
        value = grid[buffer, i, x + 1 - step_x, pl.ds(row + 8 - step_y, 8), :]
        if step_z:
            value = pltpu.roll(value, step_z % depth_z, axis=1)
        return value

    def collide_slab(step, x):
        for tile in range(tiles_y):
            row = tile * 8
            if step == 0:
                f = [f_ref[i, x, pl.ds(row, 8), :] for i in range(19)]
            else:
                f = [pulled((step - 1) % 2, i, x, row) for i in range(19)]
            relaxed, rho, u = collide_tile(f, solid_ref[x, pl.ds(row, 8), :] > 0)
            for i in range(19):
                grid[step % 2, i, x + 1, pl.ds(row + 8, 8), :] = relaxed[i]
            for n, value in enumerate([rho] + u):
                fields[n, x, pl.ds(row, 8), :] = value

    def arrive(step):
        buffer = step % 2
        for n in range(8):
            side(step, n).wait_recv()
        for k in range(5):
            grid[buffer, PLUS_X[k], 0, pl.ds(8, width_y), :] = recv_x[step, 0, k]
            grid[buffer, MINUS_X[k], width_x + 1, pl.ds(8, width_y), :] = recv_x[step, 1, k]
        for k in range(5):
            for x in range(width_x):
                line = pl.ds(k * width_x + x, 1)
                grid[buffer, PLUS_Y[k], x + 1, pl.ds(7, 1), :] = recv_y[step, 0, line, :]
                grid[buffer, MINUS_Y[k], x + 1, pl.ds(width_y + 8, 1), :] = recv_y[step, 1, line, :]
        for n, (i, step_x, step_y) in enumerate(CORNERS):
            x = 0 if step_x > 0 else width_x + 1
            row = 7 if step_y > 0 else width_y + 8
            grid[buffer, i, x, pl.ds(row, 1), :] = recv_c[step, n, pl.ds(0, 1), :]

    def sort_panels():
        owner = jnp.broadcast_to(listed_ref[pl.ds(8, 1), :], (slots, slots))
        first = lax.broadcasted_iota(jnp.int32, (slots, slots), 0).astype(jnp.float32)
        second = lax.broadcasted_iota(jnp.int32, (slots, slots), 1).astype(jnp.float32)
        earlier = (owner.T == owner) & (first < second)
        rank = jnp.sum(jnp.where(earlier, 1.0, 0.0), axis=0, keepdims=True)
        position = jnp.broadcast_to(
            listed_ref[pl.ds(8, 1), :] * float(capacity) + rank, (slots, slots)
        )
        moved = jnp.where(position.T == second, 1.0, 0.0)
        meta_ref[...] = jnp.dot(
            listed_ref[pl.ds(0, 8), :],
            moved,
            precision=lax.Precision.HIGHEST,
            preferred_element_type=jnp.float32,
        )

    cells = lax.broadcasted_iota(jnp.int32, (depth_z, slots), 0).astype(jnp.float32)
    lines = lax.broadcasted_iota(jnp.int32, (width_x * width_y, slots), 0).astype(jnp.float32)
    row_of = lax.broadcasted_iota(jnp.int32, (8, slots), 0)
    lane_of = lax.broadcasted_iota(jnp.int32, (8, 128), 1)

    def sample(step):
        at_z = jnp.where(cells == meta_ref[pl.ds(6, 1), :], 1.0, 0.0).astype(jnp.bfloat16)
        data = fields[...].reshape(4 * width_x * width_y, depth_z)
        high = data.astype(jnp.bfloat16)
        left = data - high.astype(jnp.float32)
        middle = left.astype(jnp.bfloat16)
        low = (left - middle.astype(jnp.float32)).astype(jnp.bfloat16)
        picked = sum(
            jnp.dot(part, at_z, preferred_element_type=jnp.float32) for part in (high, middle, low)
        )
        at_line = lines == meta_ref[pl.ds(3, 1), :]
        count = width_x * width_y
        rho, ux, uy, uz = (
            jnp.sum(
                jnp.where(at_line, picked[n * count : (n + 1) * count], 0.0), axis=0, keepdims=True
            )
            for n in range(4)
        )
        area = [meta_ref[pl.ds(a, 1), :] for a in range(3)]
        live = meta_ref[pl.ds(7, 1), :]
        flux = ux * area[0] + uy * area[1] + uz * area[2]
        terms = [rho * flux] + [
            (rho - 19.0) / 3.0 * a + rho * v * flux for a, v in zip(area, (ux, uy, uz))
        ]
        block = meta_ref[...] if step == 0 else jnp.zeros((8, slots), jnp.float32)
        for n in range(4):
            block = jnp.where(row_of == n, terms[n] * live, block)
        for q in range(count_x):
            start = q * capacity
            part = block[:, start // 128 * 128 : start // 128 * 128 + 128]
            shift = (step * capacity - start) % 128
            if shift:
                part = pltpu.roll(part, shift, axis=1)
            here = (lane_of >= step * capacity) & (lane_of < (step + 1) * capacity)
            old = payload[q] if step else jnp.zeros((8, 128), jnp.float32)
            payload[q] = jnp.where(here, part, old)

    def panel_copy(d):
        return pltpu.make_async_remote_copy(
            src_ref=payload.at[d // count_y],
            dst_ref=panels.at[me],
            send_sem=panel_send.at[d],
            recv_sem=panel_recv.at[me],
            device_id=(d // count_y, d % count_y),
            device_id_type=MESH,
        )

    def panel_arrival(d):
        return pltpu.make_async_remote_copy(
            src_ref=payload.at[d // count_y],
            dst_ref=panels.at[d],
            send_sem=panel_send.at[d],
            recv_sem=panel_recv.at[d],
            device_id=(d // count_y, d % count_y),
            device_id_type=MESH,
        )

    def for_others(body):
        def one(d, carry):
            @pl.when(d != me)
            def _():
                body(d)

            return carry

        lax.fori_loop(0, total, one, 0)

    for step in range(STEPS):
        buffer = step % 2
        if step:
            arrive(step - 1)
        else:
            walls.wait()
            loads[0].wait()
            loads[width_x - 1].wait()

        def outer(n, carry):
            collide_slab(step, n * (width_x - 1))
            return carry

        lax.fori_loop(0, 2, outer, 0)
        for k in range(5):
            send_x[step, 0, k] = grid[buffer, PLUS_X[k], width_x, pl.ds(8, width_y), :]
            send_x[step, 1, k] = grid[buffer, MINUS_X[k], 1, pl.ds(8, width_y), :]
        for n, (i, step_x, step_y) in enumerate(CORNERS):
            x = width_x if step_x > 0 else 1
            row = width_y + 7 if step_y > 0 else 8
            line = grid[buffer, i, x, pl.ds(row, 1), :]
            send_c[step, n] = jnp.broadcast_to(line, (8, depth_z))
        if step == 0:
            pl.semaphore_wait(barrier, total - 1)
        for n in (0, 1, 4, 5, 6, 7):
            side(step, n).start()

        if step == 0:
            for x in range(1, width_x - 1):
                loads[x].wait()

        def inner(x, carry):
            collide_slab(step, x)
            return carry

        lax.fori_loop(1, width_x - 1, inner, 0)
        for k in range(5):
            for x in range(width_x):
                line = pl.ds(k * width_x + x, 1)
                send_y[step, 0, line, :] = grid[
                    buffer, PLUS_Y[k], x + 1, pl.ds(width_y + 7, 1), :
                ]
                send_y[step, 1, line, :] = grid[buffer, MINUS_Y[k], x + 1, pl.ds(8, 1), :]
        for n in (2, 3):
            side(step, n).start()
        if step == 0:
            sort_panels()
        sample(step)

    for_others(lambda d: panel_copy(d).start())
    own = pltpu.make_async_copy(payload.at[me_x], panels.at[me], own_sem)
    own.start()
    arrive(STEPS - 1)

    def final(x, carry):
        for tile in range(tiles_y):
            for i in range(19):
                out_ref[i, x, pl.ds(tile * 8, 8), :] = pulled((STEPS - 1) % 2, i, x, tile * 8)
        return carry

    lax.fori_loop(0, width_x, final, 0)
    own.wait()
    for_others(lambda d: panel_arrival(d).wait_recv())
    panels_ref[...] = panels[...]
    for_others(lambda d: panel_copy(d).wait_send())
    for step in range(STEPS):
        for n in range(8):
            side(step, n).wait_send()


SIN_POLY = (4.44288292, -7.30824569, 3.60635422, -0.84611165, 0.10982452)
COS_POLY = (1.4142135, -6.97885095, 5.73946038, -1.88355791, 0.31068803)


def horner(poly, x):
    value = poly[-1] * x + poly[-2]
    for coefficient in poly[-3::-1]:
        value = value * x + coefficient
    return value


def spectrum_table(freq_ref, lanes):
    shape = (STEPS * 8, lanes)
    row = lax.broadcasted_iota(jnp.int32, shape, 0)
    lane = lax.broadcasted_iota(jnp.int32, shape, 1)
    step, part, column, slot = row >> 3, row & 7, lane & 7, lane >> 3
    omega = jnp.zeros(shape, jnp.float32)
    for f in range(lanes // 8):
        omega = jnp.where(slot == f, freq_ref[0, f], omega)
    taper = jnp.zeros(shape, jnp.float32)
    for s in range(STEPS):
        taper = jnp.where(
            step == s, 0.5 - 0.5 * math.cos(2.0 * math.pi * (s + 0.5) / STEPS), taper
        )
    phase = omega * step.astype(jnp.float32)
    real, imag = taper * jnp.cos(phase), -taper * jnp.sin(phase)
    wave = omega * math.sqrt(3.0)
    vector = (part >= 1) & (part <= 3)
    table = jnp.where(vector & (column == part - 1), real * wave, 0.0)
    table = jnp.where(vector & (column == part + 2), imag * wave, table)
    table = jnp.where((part == 0) & (column == 6), real * omega, table)
    return jnp.where((part == 0) & (column == 7), imag * omega, table)


def green_kernel(
    capacity, count_ref, freq_ref, panels_ref, seen_ref, out_ref, sums, samples, amplitudes
):
    freqs = freq_ref.shape[1]
    sources = panels_ref.shape[0]
    observers = seen_ref.shape[1]
    sums[...] = jnp.zeros_like(sums)
    lane_of = lax.broadcasted_iota(jnp.int32, (capacity, 128), 1)

    live = 0
    for group in range(sources // 16):
        turned = panels_ref[pl.ds(group * 16, 16)].reshape(128, 128).T
        for n in range(16):
            piece = jnp.zeros((capacity, 128), jnp.float32)
            for step in range(STEPS):
                part = turned[step * capacity : (step + 1) * capacity]
                shift = (step * 8 - n * 8) % 128
                if shift:
                    part = pltpu.roll(part, shift, axis=1)
                piece = jnp.where((lane_of >> 3) == step, part, piece)
            samples[pl.ds(live, capacity), :] = piece
            live = live + count_ref[group * 16 + n]
    samples[pl.ds(live, 8), :] = jnp.zeros((8, 128), jnp.float32)

    table = spectrum_table(freq_ref, freqs * 8)

    def transform(n, carry):
        rows = pl.ds(pl.multiple_of(n * 128, 128), 128)
        amplitudes[rows, :] = jnp.dot(
            samples[rows, :][:, : STEPS * 8],
            table,
            precision=lax.Precision.HIGHEST,
            preferred_element_type=jnp.float32,
        )
        return carry

    lax.fori_loop(0, (live + 127) // 128, transform, 0)

    def tile(n, carry):
        rows = pl.ds(pl.multiple_of(n * 8, 8), 8)
        amplitude = amplitudes[rows, :]
        coords = samples[rows, :]
        offset = [seen_ref[pl.ds(a, 1), :] - coords[:, 4 + a : 5 + a] for a in range(3)]
        distance = jnp.sqrt(
            offset[0] * offset[0] + offset[1] * offset[1] + offset[2] * offset[2]
        )
        inverse = 1.0 / distance
        toward = [value * inverse for value in offset]
        for f in range(freqs):
            column = [
                jnp.broadcast_to(amplitude[:, f * 8 + c : f * 8 + c + 1], (8, observers))
                for c in range(8)
            ]
            turns = distance * freq_ref[1, f]
            turns = turns - ((turns + 12582912.0) - 12582912.0)
            square = turns * turns
            half_sin = turns * horner(SIN_POLY, square)
            half_cos = horner(COS_POLY, square)
            cosine = 1.0 - half_sin * half_sin
            sine = half_sin * half_cos
            near = inverse * freq_ref[2, f]
            radial_re = toward[0] * column[0] + toward[1] * column[1] + toward[2] * column[2]
            radial_im = toward[0] * column[3] + toward[1] * column[4] + toward[2] * column[5]
            amp_re = radial_re * near - (radial_im + column[7])
            amp_im = radial_im * near + (radial_re + column[6])
            sums[2 * f] += inverse * (cosine * amp_re + sine * amp_im)
            sums[2 * f + 1] += inverse * (cosine * amp_im - sine * amp_re)
        return carry

    lax.fori_loop(0, (live + 7) // 8, tile, 0)
    for f in range(freqs):
        for part in range(2):
            out_ref[part, pl.ds(f, 1), :] = jnp.sum(sums[2 * f + part], axis=0, keepdims=True)


def local(
    populations, solid, panel_cell, panel_owner, panel_count, panel_area, observers, frequencies
):
    width_x, width_y, depth_z = solid.shape
    slots = panel_cell.shape[0]
    count_x, count_y = lax.axis_size("gx"), lax.axis_size("gy")
    total = count_x * count_y
    capacity = slots // count_x
    own_freq = frequencies.shape[0] // count_y
    brick_x, brick_y = lax.axis_index("gx"), lax.axis_index("gy")
    line = panel_cell // depth_z
    slot = jnp.arange(slots, dtype=jnp.int32)
    meta = jnp.stack(
        [
            panel_area[0],
            panel_area[1],
            panel_area[2],
            line.astype(jnp.float32),
            (brick_x * width_x + line // width_y).astype(jnp.float32),
            (brick_y * width_y + line % width_y).astype(jnp.float32),
            (panel_cell % depth_z).astype(jnp.float32),
            (slot < panel_count[0]).astype(jnp.float32),
        ]
        + [panel_owner.astype(jnp.float32)] * 8
    )
    f32 = jnp.float32
    vmem = pl.BlockSpec(memory_space=pltpu.VMEM)
    smem = pl.BlockSpec(memory_space=pltpu.SMEM)
    rows_y = -(-5 * width_x // 8) * 8
    flow = pl.pallas_call(
        functools.partial(flow_kernel, count_x, count_y),
        out_shape=(
            jax.ShapeDtypeStruct(populations.shape, f32),
            jax.ShapeDtypeStruct((total, 8, 128), f32),
        ),
        in_specs=[pl.BlockSpec(memory_space=pltpu.HBM)] * 2 + [vmem],
        out_specs=(vmem, vmem),
        scratch_shapes=[
            pltpu.VMEM(populations.shape, f32),
            pltpu.VMEM(solid.shape, solid.dtype),
            pltpu.VMEM((8, slots), f32),
            pltpu.SemaphoreType.DMA((width_x + 1,)),
            pltpu.VMEM((2, 19, width_x + 2, width_y + 16, depth_z), f32),
            pltpu.VMEM((4, width_x, width_y, depth_z), f32),
            pltpu.VMEM((STEPS, 2, 5, width_y, depth_z), f32),
            pltpu.VMEM((STEPS, 2, 5, width_y, depth_z), f32),
            pltpu.VMEM((STEPS, 2, rows_y, depth_z), f32),
            pltpu.VMEM((STEPS, 2, rows_y, depth_z), f32),
            pltpu.VMEM((STEPS, 4, 8, depth_z), f32),
            pltpu.VMEM((STEPS, 4, 8, depth_z), f32),
            pltpu.VMEM((count_x, 8, 128), f32),
            pltpu.VMEM((total, 8, 128), f32),
            pltpu.SemaphoreType.DMA((STEPS, 8)),
            pltpu.SemaphoreType.DMA((STEPS, 8)),
            pltpu.SemaphoreType.DMA((total,)),
            pltpu.SemaphoreType.DMA((total,)),
            pltpu.SemaphoreType.DMA,
        ],
        compiler_params=pltpu.CompilerParams(
            collective_id=0, has_side_effects=True, vmem_limit_bytes=40 * 1024 * 1024
        ),
        name="flow",
    )
    current, panels = flow(populations, solid, meta)

    own_list = lax.dynamic_slice_in_dim(frequencies, brick_y * own_freq, own_freq)
    wave = own_list * math.sqrt(3.0)
    tones = jnp.stack([own_list, wave * (0.5 / math.pi), 1.0 / wave])
    live_in = jnp.sum(panels[:, 7, :capacity], axis=1).astype(jnp.int32)
    room = (-(-(total * capacity) // 128) + 1) * 128
    spectra = pl.pallas_call(
        functools.partial(green_kernel, capacity),
        out_shape=jax.ShapeDtypeStruct((2, own_freq, observers.shape[1]), f32),
        in_specs=[smem] * 2 + [vmem] * 2,
        out_specs=vmem,
        scratch_shapes=[
            pltpu.VMEM((2 * own_freq, 8, observers.shape[1]), f32),
            pltpu.VMEM((room, 128), f32),
            pltpu.VMEM((room, own_freq * 8), f32),
        ],
        compiler_params=pltpu.CompilerParams(vmem_limit_bytes=40 * 1024 * 1024),
        name="green",
    )(live_in, tones, panels, observers)
    return (current, spectra[None])


def solution(mesh):
    return jax.shard_map(
        local,
        mesh=mesh,
        in_specs=(
            P(None, "gx", "gy", None),
            P("gx", "gy", None),
            P(("gx", "gy")),
            P(("gx", "gy")),
            P(("gx", "gy")),
            P(None, ("gx", "gy")),
            P(),
            P(),
        ),
        out_specs=(P(None, "gx", "gy", None), P("gx", None, "gy", None)),
        check_vma=False,
    )
```
